512 devices in a mesh: dp: 16 (over y, core), rule: 32 (over x, z).
Axes of the slice: x: 4, y: 8, z: 8, core: 2. Of those that a mesh axis runs over, the one named last changes fastest.
Arguments:
- hidden_states: bfloat16 [4096, 8192], P(('dp', 'rule')), may hold values from -6 to 6
- attn_input: bfloat16 [4096, 8192], P(('dp', 'rule')), may hold values from -6 to 6
- rule_ids: int32 [4096, 2], replicated, may hold values from 0 to 127, as said below
- slot_ids: int32 [4096, 2], replicated, may hold values from -1 to 127, as said below
- cotangent: bfloat16 [4096, 2], replicated, may hold values from -6 to 6
- adapter_in: bfloat16 [128, 8192, 512], P('dp', 'rule'), may hold values from -0.0625 to 0.0625
- adapter_bias: float32 [128, 512], P('dp'), may hold values from -3 to 3
- adapter_out: float32 [128, 512], P('dp'), may hold values from -0.25 to 0.25
Outputs:
- rewards: bfloat16 [4096, 2], P('dp')
- adapter_in_grad: bfloat16 [128, 8192, 512], P('dp', 'rule')
- adapter_bias_grad: float32 [128, 512], P('dp')
- adapter_out_grad: float32 [128, 512], P('dp')
- o_proj_grad: bfloat16 [8192, 8192], P('rule', 'dp')
The draws below stay inside these ranges and needn't reach their ends.
Inputs may be any that keep to these rules, and one draw needn't show every extreme that they name: `rule_ids`: the owner of rule r is r // 8. Among the 16 pairs of one block of 8 consecutive tokens at most 2 name rules of any one owner, and in every block some owner gets exactly 2. The two rules of a token differ. slot_ids[t, k] counts the earlier pairs, in the order of t then k, that name the same rule; it is -1 where that count reaches 128. Some rule fills all 128 rows.
All inputs are finite; a program needn't handle non-finite values.
Results may differ from the reference program's by a relative error of at most 0.03.
Values may be sent and summed in bfloat16 or wider, within the bound.
No kernel may reach another device: no remote copies, remote signals or barrier semaphores. Data moves between devices by JAX's collectives and lax.ppermute only.
A program may use at most 64 MiB of HBM per device.

```python
import jax
import jax.numpy as jnp
from jax import lax

D = 8192
R = 512
ADP_DEV = 8
TOK_DEV = 8
RULES = 128
TOKENS = 4096
BLOCKS = 512
GROUP = 256
GROUPS = 16
SEND = 2
CAPA = 128
N_DP = 16


def routing_draw(key):
    subkeys = jax.random.split(jax.random.fold_in(key, 17), 5)
    pair_count = 2 * TOK_DEV
    slot_count = N_DP * SEND
    hot_rule = jax.random.randint(subkeys[0], (), 0, RULES)
    hot_owner = hot_rule // ADP_DEV
    hot_local = hot_rule % ADP_DEV
    full_owner = jax.random.randint(subkeys[1], (BLOCKS, 1), 0, N_DP)
    entries = jnp.arange(slot_count)
    entry_owner = entries // SEND
    entry_rank = entries % SEND
    jitter = jax.random.randint(subkeys[2], (BLOCKS, slot_count), 0, 1 << 19)
    scores = jitter * slot_count + entries[None, :]
    scores = scores + jnp.where(entry_owner[None, :] == full_owner, 1 << 28, 0)
    scores = scores + jnp.where((entry_owner == hot_owner) & (entry_rank == 0), 1 << 27, 0)[None, :]
    _, chosen = lax.top_k(scores, pair_count)
    shuffle_key = jax.random.randint(subkeys[3], (BLOCKS, pair_count), 0, 1 << 19)
    shuffle_key = shuffle_key * pair_count + jnp.arange(pair_count)[None, :]
    ordering = jnp.argsort(shuffle_key, axis=1)
    picked = jnp.take_along_axis(chosen, ordering, axis=1)
    owner_ids = picked // SEND
    slot_rank = picked % SEND
    base_local = jax.random.randint(subkeys[4], (BLOCKS, N_DP), 0, ADP_DEV)
    base_local = jnp.where(jnp.arange(N_DP)[None, :] == hot_owner, hot_local, base_local)
    local_ids = (jnp.take_along_axis(base_local, owner_ids, axis=1) + slot_rank) % ADP_DEV
    return (owner_ids * ADP_DEV + local_ids).reshape(TOKENS, 2).astype(jnp.int32)


def draw_rule_ids(key, part):
    return routing_draw(key)


def draw_slot_ids(key, part):
    flat_rules = routing_draw(key).reshape(-1)
    one_hot = (flat_rules[:, None] == jnp.arange(RULES)[None, :]).astype(jnp.int32)
    earlier = jnp.cumsum(one_hot, axis=0) - one_hot
    counted = jnp.sum(earlier * one_hot, axis=1)
    return jnp.where(counted < CAPA, counted, -1).reshape(TOKENS, 2).astype(jnp.int32)


def levels(key, shape, shards, least, high):
    def one(dim, parts):
        steps = jax.random.uniform(jax.random.fold_in(jax.random.fold_in(key, 6), dim), (parts,), jnp.float32, least / len(shards), high / len(shards))
        return jnp.repeat(jnp.exp(steps), shape[dim] // parts).reshape((-1,) + (1,) * (len(shape) - dim - 1))

    level = one(*shards[0])
    for cut in shards[1:]:
        level = level * one(*cut)
    return level


def normal_values(stream_key, dims, deviation, bound, cuts=(), held_as=jnp.bfloat16):
    drawn = jax.random.normal(stream_key, dims, jnp.float32) * deviation
    if len(cuts) > 0:
        drawn = levels(stream_key, dims, cuts, -0.22, 0.18) * drawn
    return jnp.clip(drawn, min=-bound, max=bound).astype(held_as)


def setup_inputs(seed: int = 0) -> dict:
    key_list = jax.random.split(jax.random.key(seed), 9)
    return {
        "hidden_states": normal_values(key_list[0], (TOKENS, D), 1.0, 6.0, ((0, 512),)),
        "attn_input": normal_values(key_list[1], (TOKENS, D), 1.0, 6.0, ((0, 512),)),
        "rule_ids": draw_rule_ids(jax.random.fold_in(key_list[8], 71), 0),
        "slot_ids": draw_slot_ids(jax.random.fold_in(key_list[8], 71), 0),
        "cotangent": normal_values(key_list[4], (TOKENS, 2), 1.0, 6.0),
        "adapter_in": normal_values(key_list[5], (RULES, D, R), D ** -0.5, 0.0625, ((0, 16), (1, 32))),
        "adapter_bias": normal_values(key_list[6], (RULES, R), 0.5, 3.0, ((0, 16),), jnp.float32),
        "adapter_out": normal_values(key_list[7], (RULES, R), R ** -0.5, 0.25, ((0, 16),), jnp.float32),
    }


def adapter_pass(inputs):
    rows_in, weight_in, bias_in, weight_out, cot_rows = inputs
    preact = jnp.dot(rows_in, weight_in, preferred_element_type=jnp.float32) + bias_in
    sigmoid_z = jax.nn.sigmoid(preact)
    activated = preact * sigmoid_z
    reward_rows = jnp.sum(activated * weight_out, axis=1)
    grad_pre = cot_rows[:, None] * weight_out * sigmoid_z * (1.0 + preact * (1.0 - sigmoid_z))
    grad_half = grad_pre.astype(jnp.bfloat16)
    weight_grad = jnp.dot(rows_in.T, grad_half, preferred_element_type=jnp.float32).astype(jnp.bfloat16)
    bias_grad = jnp.sum(grad_pre, axis=0)
    out_grad = jnp.sum(cot_rows[:, None] * activated, axis=0)
    input_grad = jnp.dot(grad_half, weight_in.T, preferred_element_type=jnp.float32).astype(jnp.bfloat16)
    return reward_rows, weight_grad, bias_grad, out_grad, input_grad


def reference(hidden_states, attn_input, rule_ids, slot_ids, cotangent, adapter_in, adapter_bias, adapter_out):
    flat_rules = rule_ids.reshape(-1).astype(jnp.int32)
    flat_slots = slot_ids.reshape(-1).astype(jnp.int32)
    dump_row = RULES * CAPA
    position = jnp.where(flat_slots >= 0, flat_rules * CAPA + flat_slots, dump_row).astype(jnp.int32)
    token_of = (jnp.arange(2 * TOKENS) // 2).astype(jnp.int32)
    buffers = jnp.zeros((dump_row + 1, D), jnp.bfloat16).at[position].set(hidden_states[token_of])
    buffers = buffers[:dump_row].reshape(RULES, CAPA, D)
    cot_buffers = jnp.zeros((dump_row + 1,), jnp.float32).at[position].set(cotangent.reshape(-1).astype(jnp.float32))
    cot_buffers = cot_buffers[:dump_row].reshape(RULES, CAPA)
    reward_buf, in_grad, bias_grad, out_grad, input_grad = lax.map(
        adapter_pass, (buffers, adapter_in, adapter_bias, adapter_out, cot_buffers))
    reward_flat = jnp.concatenate([reward_buf.reshape(-1), jnp.zeros((1,), jnp.float32)])
    rewards = reward_flat[position].reshape(TOKENS, 2).astype(jnp.bfloat16)
    grad_flat = jnp.concatenate([input_grad.reshape(dump_row, D), jnp.zeros((1, D), jnp.bfloat16)])
    pair_grads = grad_flat[position].astype(jnp.float32).reshape(TOKENS, 2, D)
    state_grad = jnp.sum(pair_grads, axis=1).astype(jnp.bfloat16)
    grads_by_group = state_grad.reshape(GROUPS, GROUP, D)
    attn_by_group = attn_input.reshape(GROUPS, GROUP, D)

    def add_group(total_sum, inputs):
        grad_rows, attn_rows = inputs
        partial_sum = jnp.dot(grad_rows.T, attn_rows, preferred_element_type=jnp.float32)
        rounded = lax.optimization_barrier(partial_sum.astype(jnp.bfloat16))
        return total_sum + rounded.astype(jnp.float32), None

    total_sum, _ = lax.scan(add_group, jnp.zeros((D, D), jnp.float32), (grads_by_group, attn_by_group))
    return rewards, in_grad, bias_grad, out_grad, total_sum.astype(jnp.bfloat16)
```

```python
import functools

import jax
import jax.numpy as jnp
from jax import lax
from jax.experimental import pallas as pl
from jax.experimental.pallas import tpu as pltpu
from jax.sharding import PartitionSpec as P

BF16 = jnp.bfloat16
F32 = jnp.float32
NN = (((1,), (0,)), ((), ()))
NT = (((1,), (1,)), ((), ()))
TN = (((0,), (0,)), ((), ()))


def mm(a, b, dims=NN):
    return lax.dot_general(a, b, dims, preferred_element_type=F32)


def tables_kernel(block, me_ref, owner_ref, pos_ref, cot_ref, sort_ref, unsort_ref, pick_ref, cot_out_ref):
    me = me_ref[0]
    groups, tokens = owner_ref.shape[1:]
    rows = sort_ref.shape[0]
    slots = 2 * (tokens // block)
    owner = [owner_ref[k] for k in range(2)]
    pos = [pos_ref[k] for k in range(2)]
    cot = [cot_ref[k].astype(F32) for k in range(2)]
    token = lax.broadcasted_iota(jnp.int32, (groups, tokens), 1)
    in_block = token % block
    rank = [jnp.zeros((groups, tokens), jnp.int32), (owner[0] == owner[1]).astype(jnp.int32)]
    for shift in range(1, block):
        for other in range(2):
            moved = pltpu.roll(owner[other], shift, 1)
            for k in range(2):
                hit = (moved == owner[k]) & (in_block >= shift)
                rank[k] = rank[k] + hit.astype(jnp.int32)
    place = [2 * (token // block) + rank[k] for k in range(2)]
    held = [pos[k] >= 0 for k in range(2)]

    mine = lax.broadcasted_iota(jnp.int32, (groups, tokens), 0) == me
    slot_row = lax.broadcasted_iota(jnp.int32, (groups * slots, tokens), 0)
    for k in range(2):
        key = jnp.where(held[k], owner[k] * slots + place[k], -1)
        key = jnp.sum(jnp.where(mine, key, 0), axis=0, keepdims=True)
        pick_ref[k] = jnp.where(slot_row == key, 1.0, 0.0).astype(BF16)

    received = [jnp.where(held[k] & (owner[k] == me), place[k], -1) for k in range(2)]
    high = [((pos[k] + 1) // 32).astype(F32).astype(BF16) for k in range(2)]
    low = [((pos[k] + 1) % 32).astype(F32).astype(BF16) for k in range(2)]
    cot = [cot[k].astype(BF16) for k in range(2)]
    pair = 128 // slots
    cot_total = jnp.zeros((rows, 128), F32)
    lane_row = lax.broadcasted_iota(jnp.int32, (128, tokens), 0)
    buffer_row = lax.broadcasted_iota(jnp.int32, (rows, 128), 0)
    buffer_lane = lax.broadcasted_iota(jnp.int32, (128, rows), 1)
    for step in range(groups // pair):
        ones, highs, lows, cots = [], [], [], []
        for part in range(pair):
            g = step * pair + part
            for k in range(2):
                row = received[k][g : g + 1]
                row = jnp.where(row >= 0, row + part * slots, -1)
                ones.append(jnp.where(lane_row == row, 1.0, 0.0).astype(BF16))
                highs.append(high[k][g : g + 1])
                lows.append(low[k][g : g + 1])
                cots.append(cot[k][g : g + 1])
        chosen = jnp.concatenate(ones, axis=1)
        wide = chosen.shape[1]
        high_row = jnp.broadcast_to(jnp.concatenate(highs, axis=1), (128, wide))
        low_row = jnp.broadcast_to(jnp.concatenate(lows, axis=1), (128, wide))
        cot_row = jnp.broadcast_to(jnp.concatenate(cots, axis=1), (128, wide))
        at_lane = (mm(high_row, chosen, NT) * 32.0 + mm(low_row, chosen, NT)).astype(jnp.int32) - 1
        at_row = (mm(chosen, high_row, NT) * 32.0 + mm(chosen, low_row, NT)).astype(jnp.int32) - 1
        cot_lane = mm(cot_row, chosen, NT).astype(BF16)
        hit = jnp.where(buffer_row == at_lane[0:1], 1.0, 0.0).astype(BF16)
        sort_ref[:, step * 128 : (step + 1) * 128] = hit
        cot_total = cot_total + mm(hit, cot_lane, NT)
        at_row = jnp.concatenate([at_row] * (rows // 128), axis=1)
        unsort_ref[step * 128 : (step + 1) * 128, :] = jnp.where(buffer_lane == at_row, 1.0, 0.0).astype(BF16)
    cot_out_ref[...] = cot_total


def tables(block, rows, me, owner, pos, cot):
    groups, tokens = owner.shape[1:]
    received = groups * 2 * (tokens // block)
    vmem = pl.BlockSpec(memory_space=pltpu.VMEM)
    return pl.pallas_call(
        functools.partial(tables_kernel, block),
        out_shape=(
            jax.ShapeDtypeStruct((rows, received), BF16),
            jax.ShapeDtypeStruct((received, rows), BF16),
            jax.ShapeDtypeStruct((2, received, tokens), BF16),
            jax.ShapeDtypeStruct((rows, 128), F32),
        ),
        in_specs=[pl.BlockSpec(memory_space=pltpu.SMEM), vmem, vmem, vmem],
        out_specs=(vmem, vmem, vmem, vmem),
        compiler_params=pltpu.CompilerParams(vmem_limit_bytes=32 * 2**20),
        cost_estimate=pl.CostEstimate(flops=10**9, bytes_accessed=6 * 2**20, transcendentals=0),
    )(me, owner, pos, cot)


def forward_kernel(sort_ref, got_ref, weight_ref, rows_ref, part_ref):
    rows = mm(sort_ref[...], got_ref[...]).astype(BF16)
    rows_ref[...] = rows
    part_ref[...] = mm(rows, weight_ref[0]).astype(BF16)


def forward(sort, got, weight):
    adapters, features, hidden = weight.shape
    rows, received = sort.shape
    capacity = rows // adapters
    return pl.pallas_call(
        forward_kernel,
        grid=(adapters,),
        out_shape=(
            jax.ShapeDtypeStruct((rows, features), BF16),
            jax.ShapeDtypeStruct((rows, hidden), BF16),
        ),
        in_specs=[
            pl.BlockSpec((capacity, received), lambda a: (a, 0)),
            pl.BlockSpec((received, features), lambda a: (0, 0)),
            pl.BlockSpec((1, features, hidden), lambda a: (a, 0, 0)),
        ],
        out_specs=(
            pl.BlockSpec((capacity, features), lambda a: (a, 0)),
            pl.BlockSpec((capacity, hidden), lambda a: (a, 0)),
        ),
        compiler_params=pltpu.CompilerParams(vmem_limit_bytes=32 * 2**20),
        cost_estimate=pl.CostEstimate(flops=10**9, bytes_accessed=6 * 2**20, transcendentals=0),
    )(sort, got, weight)


def backward_kernel(
    pre_ref, bias_ref, out_ref, cot_ref, weight_ref, unsort_ref,
    half_ref, bias_grad_ref, out_grad_ref, back_ref, reward_ref, grads,
):
    a = pl.program_id(0)
    capacity, hidden = pre_ref.shape
    features = weight_ref.shape[1]
    read_out = out_ref[0]
    pre = pre_ref[...].astype(F32) + bias_ref[0]
    s = 1.0 / (1.0 + jnp.exp(-pre))
    cot = jnp.concatenate([cot_ref[...]] * (hidden // 128), axis=1)
    activated = pre * s
    grad_pre = cot * read_out * s * (1.0 + pre * (1.0 - s))
    half = grad_pre.astype(BF16)
    half_ref[...] = half
    bias_grad_ref[0] = jnp.sum(grad_pre, axis=0, keepdims=True)
    out_grad_ref[0] = jnp.sum(cot * activated, axis=0, keepdims=True)
    reward = jnp.sum(activated * read_out, axis=1, keepdims=True)
    at = pl.ds(pl.multiple_of(a * capacity, capacity), capacity)
    grads[at, :features] = mm(half, weight_ref[0], NT).astype(BF16)
    grads[at, features:] = jnp.broadcast_to(reward, (capacity, 128)).astype(BF16)

    @pl.when(a == pl.num_programs(0) - 1)
    def _():
        back = mm(unsort_ref[...], grads[...]).astype(BF16)
        back_ref[...] = back[:, :features]
        first = lax.broadcasted_iota(jnp.int32, (16, 128), 1) == 0
        first = jnp.where(first, 1.0, 0.0).astype(BF16)
        reward_ref[...] = mm(first, back[:, features:], NT).astype(BF16)


def backward(pre, bias, read_out, cot, weight, unsort):
    adapters, features, hidden = weight.shape
    received, rows = unsort.shape
    capacity = rows // adapters
    line = pl.BlockSpec((1, 1, hidden), lambda a: (a, 0, 0))
    half, bias_grad, out_grad, back, reward = pl.pallas_call(
        backward_kernel,
        grid=(adapters,),
        out_shape=(
            jax.ShapeDtypeStruct((rows, hidden), BF16),
            jax.ShapeDtypeStruct((adapters, 1, hidden), F32),
            jax.ShapeDtypeStruct((adapters, 1, hidden), F32),
            jax.ShapeDtypeStruct((received, features), BF16),
            jax.ShapeDtypeStruct((16, received), BF16),
        ),
        in_specs=[
            pl.BlockSpec((capacity, hidden), lambda a: (a, 0)),
            line,
            line,
            pl.BlockSpec((capacity, 128), lambda a: (a, 0)),
            pl.BlockSpec((1, features, hidden), lambda a: (a, 0, 0)),
            pl.BlockSpec((received, rows), lambda a: (0, 0)),
        ],
        out_specs=(
            pl.BlockSpec((capacity, hidden), lambda a: (a, 0)),
            line,
            line,
            pl.BlockSpec((received, features), lambda a: (0, 0)),
            pl.BlockSpec((16, received), lambda a: (0, 0)),
        ),
        scratch_shapes=[pltpu.VMEM((rows, features + 128), BF16)],
        compiler_params=pltpu.CompilerParams(vmem_limit_bytes=32 * 2**20),
        cost_estimate=pl.CostEstimate(flops=10**9, bytes_accessed=8 * 2**20, transcendentals=2**19),
    )(pre, bias[:, None], read_out[:, None], cot, weight, unsort)
    return half, bias_grad[:, 0], out_grad[:, 0], back, reward


def local(
    hidden_states, attn_input, rule_ids, slot_ids, cotangent, adapter_in, adapter_bias, adapter_out
):
    dp_size = lax.axis_size("dp")
    rule_size = lax.axis_size("rule")
    block = hidden_states.shape[0]
    adapters, feature_cols, hidden_units = adapter_in.shape
    tokens = block * rule_size
    capacity = 4 * block * rule_size // adapters
    rows = adapters * capacity
    slots = 2 * rule_size

    group_rows = lax.all_to_all(hidden_states, "rule", split_axis=1, concat_axis=0, tiled=True)
    attn_cols = lax.all_to_all(attn_input, "dp", split_axis=1, concat_axis=0, tiled=True)
    attn_all = lax.all_gather(
        attn_cols.reshape(dp_size, block, -1), "rule", axis=1, tiled=True
    ).reshape(dp_size * tokens, -1)

    rule_all = rule_ids.T.reshape(2, dp_size, tokens)
    slot_all = slot_ids.T.reshape(2, dp_size, tokens)
    cot_all = cotangent.T.reshape(2, dp_size, tokens)
    owner = rule_all // adapters
    pos = jnp.where(slot_all >= 0, rule_all % adapters * capacity + slot_all, -1)
    me = lax.axis_index("dp").astype(jnp.int32).reshape(1)
    sort, unsort, pick, cot_rows = tables(block, rows, me, owner, pos, cot_all)
    pick_sum = pick[0] + pick[1]

    outgoing = mm(pick_sum, group_rows).astype(BF16)
    got = lax.all_to_all(outgoing, "dp", split_axis=0, concat_axis=0, tiled=True)
    rows_buf, partial_pre = forward(sort, got, adapter_in)
    shares = lax.all_to_all(partial_pre, "rule", split_axis=0, concat_axis=0, tiled=True)
    share = jnp.sum(
        shares.reshape(rule_size, rows // rule_size, hidden_units).astype(F32), axis=0
    ).astype(BF16)
    share = jnp.broadcast_to(share[None], (rule_size,) + share.shape).reshape(rows, hidden_units)
    preact = lax.all_to_all(share, "rule", split_axis=0, concat_axis=0, tiled=True)

    grad_half, bias_grad, out_grad, back, reward = backward(
        preact, adapter_bias, adapter_out, cot_rows, adapter_in, unsort
    )
    returned = lax.all_to_all(back, "dp", split_axis=0, concat_axis=0, tiled=True)
    state_grad = mm(pick_sum, returned, TN).astype(BF16)
    state_all = lax.all_gather(state_grad, "dp", axis=0, tiled=True)

    reward_back = lax.all_to_all(
        reward[0].reshape(dp_size, slots), "dp", split_axis=0, concat_axis=0, tiled=True
    )
    rewards = lax.dot_general(
        pick, reward_back.reshape(-1), (((1,), (0,)), ((), ())), preferred_element_type=F32
    )
    rewards = rewards.astype(BF16).T
    in_grad = jnp.einsum(
        "acd,acr->adr",
        rows_buf.reshape(adapters, capacity, feature_cols),
        grad_half.reshape(adapters, capacity, hidden_units),
        preferred_element_type=F32,
    ).astype(BF16)
    o_proj_grad = mm(state_all, attn_all, TN).astype(BF16)
    return (rewards, in_grad, bias_grad, out_grad, o_proj_grad)


def solution(mesh):
    placed = (
        P(("dp", "rule"), None),
        P(("dp", "rule"), None),
        P(),
        P(),
        P(),
        P("dp", "rule", None),
        P("dp", None),
        P("dp", None),
    )
    return jax.shard_map(
        local,
        mesh=mesh,
        in_specs=placed,
        out_specs=(
            P("dp", None),
            P("dp", "rule", None),
            P("dp", None),
            P("dp", None),
            P("rule", "dp"),
        ),
        check_vma=False,
    )
```

```python
import functools

import jax
import jax.numpy as jnp
from jax import lax
from jax.experimental import pallas as pl
from jax.experimental.pallas import tpu as pltpu
from jax.sharding import PartitionSpec as P

BF16 = jnp.bfloat16
F32 = jnp.float32
NN = (((1,), (0,)), ((), ()))
NT = (((1,), (1,)), ((), ()))
TN = (((0,), (0,)), ((), ()))


def mm(a, b, dims=NN):
    return lax.dot_general(a, b, dims, preferred_element_type=F32)


def tables_kernel(block, me_ref, owner_ref, pos_ref, cot_ref, sort_ref, unsort_ref, pick_ref, cot_out_ref):
    me = me_ref[0]
    groups, tokens = owner_ref.shape[1:]
    rows = sort_ref.shape[0]
    slots = 2 * (tokens // block)
    owner = [owner_ref[k] for k in range(2)]
    pos = [pos_ref[k] for k in range(2)]
    cot = [cot_ref[k].astype(F32) for k in range(2)]
    token = lax.broadcasted_iota(jnp.int32, (groups, tokens), 1)
    in_block = token % block
    rank = [jnp.zeros((groups, tokens), jnp.int32), (owner[0] == owner[1]).astype(jnp.int32)]
    for shift in range(1, block):
        for other in range(2):
            moved = pltpu.roll(owner[other], shift, 1)
            for k in range(2):
                hit = (moved == owner[k]) & (in_block >= shift)
                rank[k] = rank[k] + hit.astype(jnp.int32)
    place = [2 * (token // block) + rank[k] for k in range(2)]
    held = [pos[k] >= 0 for k in range(2)]

    mine = lax.broadcasted_iota(jnp.int32, (groups, tokens), 0) == me
    slot_row = lax.broadcasted_iota(jnp.int32, (groups * slots, tokens), 0)
    for k in range(2):
        key = jnp.where(held[k], owner[k] * slots + place[k], -1)
        key = jnp.sum(jnp.where(mine, key, 0), axis=0, keepdims=True)
        pick_ref[k] = jnp.where(slot_row == key, 1.0, 0.0).astype(BF16)

    received = [jnp.where(held[k] & (owner[k] == me), place[k], -1) for k in range(2)]
    high = [((pos[k] + 1) // 32).astype(F32).astype(BF16) for k in range(2)]
    low = [((pos[k] + 1) % 32).astype(F32).astype(BF16) for k in range(2)]
    cot = [cot[k].astype(BF16) for k in range(2)]
    pair = 128 // slots
    cot_total = jnp.zeros((rows, 128), F32)
    lane_row = lax.broadcasted_iota(jnp.int32, (128, tokens), 0)
    buffer_row = lax.broadcasted_iota(jnp.int32, (rows, 128), 0)
    buffer_lane = lax.broadcasted_iota(jnp.int32, (128, rows), 1)
    for step in range(groups // pair):
        ones, highs, lows, cots = [], [], [], []
        for part in range(pair):
            g = step * pair + part
            for k in range(2):
                row = received[k][g : g + 1]
                row = jnp.where(row >= 0, row + part * slots, -1)
                ones.append(jnp.where(lane_row == row, 1.0, 0.0).astype(BF16))
                highs.append(high[k][g : g + 1])
                lows.append(low[k][g : g + 1])
                cots.append(cot[k][g : g + 1])
        chosen = jnp.concatenate(ones, axis=1)
        wide = chosen.shape[1]
        high_row = jnp.broadcast_to(jnp.concatenate(highs, axis=1), (128, wide))
        low_row = jnp.broadcast_to(jnp.concatenate(lows, axis=1), (128, wide))
        cot_row = jnp.broadcast_to(jnp.concatenate(cots, axis=1), (128, wide))
        at_lane = (mm(high_row, chosen, NT) * 32.0 + mm(low_row, chosen, NT)).astype(jnp.int32) - 1
        at_row = (mm(chosen, high_row, NT) * 32.0 + mm(chosen, low_row, NT)).astype(jnp.int32) - 1
        cot_lane = mm(cot_row, chosen, NT).astype(BF16)
        hit = jnp.where(buffer_row == at_lane[0:1], 1.0, 0.0).astype(BF16)
        sort_ref[:, step * 128 : (step + 1) * 128] = hit
        cot_total = cot_total + mm(hit, cot_lane, NT)
        at_row = jnp.concatenate([at_row] * (rows // 128), axis=1)
        unsort_ref[step * 128 : (step + 1) * 128, :] = jnp.where(buffer_lane == at_row, 1.0, 0.0).astype(BF16)
    cot_out_ref[...] = cot_total


def tables(block, rows, me, owner, pos, cot):
    groups, tokens = owner.shape[1:]
    received = groups * 2 * (tokens // block)
    vmem = pl.BlockSpec(memory_space=pltpu.VMEM)
    return pl.pallas_call(
        functools.partial(tables_kernel, block),
        out_shape=(
            jax.ShapeDtypeStruct((rows, received), BF16),
            jax.ShapeDtypeStruct((received, rows), BF16),
            jax.ShapeDtypeStruct((2, received, tokens), BF16),
            jax.ShapeDtypeStruct((rows, 128), F32),
        ),
        in_specs=[pl.BlockSpec(memory_space=pltpu.SMEM), vmem, vmem, vmem],
        out_specs=(vmem, vmem, vmem, vmem),
        compiler_params=pltpu.CompilerParams(vmem_limit_bytes=16 * 2**20),
        cost_estimate=pl.CostEstimate(flops=10**9, bytes_accessed=6 * 2**20, transcendentals=0),
    )(me, owner, pos, cot)


def forward_kernel(sort_ref, got_ref, weight_ref, rows_ref, part_ref, attn_ref):
    groups, height, features = got_ref.shape
    slots = sort_ref.shape[1] // groups
    got = got_ref[:, :slots].reshape(groups * slots, features)
    rows = mm(sort_ref[...], got).astype(BF16)
    rows_ref[...] = rows
    part_ref[...] = mm(rows, weight_ref[0]).astype(BF16)

    @pl.when(pl.program_id(0) == 0)
    def _():
        block = attn_ref.shape[1]
        attn_ref[:, :, :features] = got_ref[:, slots : slots + block]
        attn_ref[:, :, features:] = got_ref[:, slots + block :]


def forward(sort, got, weight):
    adapters, features, hidden = weight.shape
    rows, received = sort.shape
    capacity = rows // adapters
    slots = received // got.shape[0]
    attn = (got.shape[0], (got.shape[1] - slots) // 2, 2 * features)
    return pl.pallas_call(
        forward_kernel,
        grid=(adapters,),
        out_shape=(
            jax.ShapeDtypeStruct((rows, features), BF16),
            jax.ShapeDtypeStruct((rows, hidden), BF16),
            jax.ShapeDtypeStruct(attn, BF16),
        ),
        in_specs=[
            pl.BlockSpec((capacity, received), lambda a: (a, 0)),
            pl.BlockSpec(got.shape, lambda a: (0, 0, 0)),
            pl.BlockSpec((1, features, hidden), lambda a: (a, 0, 0)),
        ],
        out_specs=(
            pl.BlockSpec((capacity, features), lambda a: (a, 0)),
            pl.BlockSpec((capacity, hidden), lambda a: (a, 0)),
            pl.BlockSpec(attn, lambda a: (0, 0, 0)),
        ),
        compiler_params=pltpu.CompilerParams(vmem_limit_bytes=58 * 2**20),
        cost_estimate=pl.CostEstimate(flops=10**9, bytes_accessed=6 * 2**20, transcendentals=0),
    )(sort, got, weight)


def backward_kernel(
    pre_ref, bias_ref, out_ref, cot_ref, weight_ref, unsort_ref,
    half_ref, bias_grad_ref, out_grad_ref, back_ref, reward_ref, grads,
):
    a = pl.program_id(0)
    capacity, hidden = pre_ref.shape
    features = weight_ref.shape[1]
    read_out = out_ref[0]
    pre = pre_ref[...].astype(F32) + bias_ref[0]
    s = 1.0 / (1.0 + jnp.exp(-pre))
    cot = jnp.concatenate([cot_ref[...]] * (hidden // 128), axis=1)
    activated = pre * s
    grad_pre = cot * read_out * s * (1.0 + pre * (1.0 - s))
    half = grad_pre.astype(BF16)
    half_ref[...] = half
    bias_grad_ref[0] = jnp.sum(grad_pre, axis=0, keepdims=True)
    out_grad_ref[0] = jnp.sum(cot * activated, axis=0, keepdims=True)
    reward = jnp.sum(activated * read_out, axis=1, keepdims=True)
    at = pl.ds(pl.multiple_of(a * capacity, capacity), capacity)
    grads[at, :features] = mm(half, weight_ref[0], NT).astype(BF16)
    grads[at, features:] = jnp.broadcast_to(reward, (capacity, 128)).astype(BF16)

    @pl.when(a == pl.num_programs(0) - 1)
    def _():
        back = mm(unsort_ref[...], grads[...]).astype(BF16)
        back_ref[...] = back[:, :features]
        first = lax.broadcasted_iota(jnp.int32, (16, 128), 1) == 0
        first = jnp.where(first, 1.0, 0.0).astype(BF16)
        reward_ref[...] = mm(first, back[:, features:], NT).astype(BF16)


def backward(pre, bias, read_out, cot, weight, unsort):
    adapters, features, hidden = weight.shape
    received, rows = unsort.shape
    capacity = rows // adapters
    line = pl.BlockSpec((1, 1, hidden), lambda a: (a, 0, 0))
    half, bias_grad, out_grad, back, reward = pl.pallas_call(
        backward_kernel,
        grid=(adapters,),
        out_shape=(
            jax.ShapeDtypeStruct((rows, hidden), BF16),
            jax.ShapeDtypeStruct((adapters, 1, hidden), F32),
            jax.ShapeDtypeStruct((adapters, 1, hidden), F32),
            jax.ShapeDtypeStruct((received, features), BF16),
            jax.ShapeDtypeStruct((16, received), BF16),
        ),
        in_specs=[
            pl.BlockSpec((capacity, hidden), lambda a: (a, 0)),
            line,
            line,
            pl.BlockSpec((capacity, 128), lambda a: (a, 0)),
            pl.BlockSpec((1, features, hidden), lambda a: (a, 0, 0)),
            pl.BlockSpec((received, rows), lambda a: (0, 0)),
        ],
        out_specs=(
            pl.BlockSpec((capacity, hidden), lambda a: (a, 0)),
            line,
            line,
            pl.BlockSpec((received, features), lambda a: (0, 0)),
            pl.BlockSpec((16, received), lambda a: (0, 0)),
        ),
        scratch_shapes=[pltpu.VMEM((rows, features + 128), BF16)],
        compiler_params=pltpu.CompilerParams(vmem_limit_bytes=58 * 2**20),
        cost_estimate=pl.CostEstimate(flops=10**9, bytes_accessed=8 * 2**20, transcendentals=2**19),
    )(pre, bias[:, None], read_out[:, None], cot, weight, unsort)
    return half, bias_grad[:, 0], out_grad[:, 0], back, reward


def pick_kernel(pick_ref, group_ref, attn_ref, out_ref):
    owners, height, features = out_ref.shape
    block = attn_ref.shape[0]
    slots = height - 2 * block
    chosen = pick_ref[0] + pick_ref[1]
    out = mm(chosen, group_ref[...]).astype(BF16)
    out_ref[:, :slots] = out.reshape(owners, slots, features)
    for o in range(owners):
        start = 2 * o * features
        left = attn_ref[:, start : start + features]
        right = attn_ref[:, start + features : start + 2 * features]
        out_ref[o, slots:] = jnp.concatenate([left, right], axis=0)


def call(kernel, outs, mflops, mbytes, *args):
    vmem = pl.BlockSpec(memory_space=pltpu.VMEM)
    smem = pl.BlockSpec(memory_space=pltpu.SMEM)
    return pl.pallas_call(
        kernel,
        out_shape=tuple(jax.ShapeDtypeStruct(shape, dtype) for shape, dtype in outs),
        in_specs=[smem if arg.ndim == 1 else vmem for arg in args],
        out_specs=tuple(vmem for _ in outs),
        compiler_params=pltpu.CompilerParams(vmem_limit_bytes=12 * 2**20),
        cost_estimate=pl.CostEstimate(
            flops=mflops * 10**6, bytes_accessed=mbytes * 2**20, transcendentals=0
        ),
    )(*args)


def local(
    hidden_states, attn_input, rule_ids, slot_ids, cotangent, adapter_in, adapter_bias, adapter_out
):
    dp_size = lax.axis_size("dp")
    rule_size = lax.axis_size("rule")
    block = hidden_states.shape[0]
    adapters, feature_cols, hidden_units = adapter_in.shape
    tokens = block * rule_size
    capacity = 4 * block * rule_size // adapters
    rows = adapters * capacity
    slots = 2 * rule_size

    group_rows = lax.all_to_all(hidden_states, "rule", split_axis=1, concat_axis=0, tiled=True)

    rule_all = rule_ids.T.reshape(2, dp_size, tokens)
    slot_all = slot_ids.T.reshape(2, dp_size, tokens)
    cot_all = cotangent.T.reshape(2, dp_size, tokens)
    owner = rule_all // adapters
    pos = jnp.where(slot_all >= 0, rule_all % adapters * capacity + slot_all, -1)
    me = lax.axis_index("dp").astype(jnp.int32).reshape(1)
    sort, unsort, pick, cot_rows = tables(block, rows, me, owner, pos, cot_all)
    (outgoing,) = call(
        pick_kernel, [((dp_size, slots + 2 * block, feature_cols), BF16)], 200, 2,
        pick, group_rows, attn_input,
    )
    got = lax.all_to_all(outgoing, "dp", split_axis=0, concat_axis=0, tiled=True)
    rows_buf, partial_pre, attn_cols = forward(sort, got, adapter_in)
    attn_all = lax.all_gather(attn_cols, "rule", axis=1, tiled=True)
    attn_all = attn_all.reshape(dp_size * tokens, -1)
    shares = lax.all_to_all(partial_pre, "rule", split_axis=0, concat_axis=0, tiled=True)
    share = jnp.sum(
        shares.reshape(rule_size, rows // rule_size, hidden_units).astype(F32), axis=0
    ).astype(BF16)
    share = jnp.broadcast_to(share[None], (rule_size,) + share.shape).reshape(rows, hidden_units)
    preact = lax.all_to_all(share, "rule", split_axis=0, concat_axis=0, tiled=True)

    grad_half, bias_grad, out_grad, back, reward = backward(
        preact, adapter_bias, adapter_out, cot_rows, adapter_in, unsort
    )
    returned = lax.all_to_all(back, "dp", split_axis=0, concat_axis=0, tiled=True)
    state_grad = mm(pick[0] + pick[1], returned, TN).astype(BF16)
    attn_all, state_grad = lax.optimization_barrier((attn_all, state_grad))
    state_all = lax.all_gather(state_grad, "dp", axis=0, tiled=True)

    reward_back = lax.all_to_all(
        reward[0].reshape(dp_size, slots), "dp", split_axis=0, concat_axis=0, tiled=True
    )
    rewards = lax.dot_general(
        pick, reward_back.reshape(-1), (((1,), (0,)), ((), ())), preferred_element_type=F32
    )
    rewards = rewards.astype(BF16).T
    in_grad = jnp.einsum(
        "acd,acr->adr",
        rows_buf.reshape(adapters, capacity, feature_cols),
        grad_half.reshape(adapters, capacity, hidden_units),
        preferred_element_type=F32,
    ).astype(BF16)
    o_proj_grad = mm(state_all, attn_all, TN).astype(BF16)
    return (rewards, in_grad, bias_grad, out_grad, o_proj_grad)


def solution(mesh):
    placed = (
        P(("dp", "rule"), None),
        P(("dp", "rule"), None),
        P(),
        P(),
        P(),
        P("dp", "rule", None),
        P("dp", None),
        P("dp", None),
    )
    return jax.shard_map(
        local,
        mesh=mesh,
        in_specs=placed,
        out_specs=(
            P("dp", None),
            P("dp", "rule", None),
            P("dp", None),
            P("dp", None),
            P("rule", "dp"),
        ),
        check_vma=False,
    )
```

```python
import functools

import jax
import jax.numpy as jnp
from jax import lax
from jax.experimental import pallas as pl
from jax.experimental.pallas import tpu as pltpu
from jax.sharding import PartitionSpec as P

BF16 = jnp.bfloat16
F32 = jnp.float32
NN = (((1,), (0,)), ((), ()))
NT = (((1,), (1,)), ((), ()))
TN = (((0,), (0,)), ((), ()))


def mm(a, b, dims=NN):
    return lax.dot_general(a, b, dims, preferred_element_type=F32)


def tables_kernel(block, me_ref, owner_ref, pos_ref, cot_ref, sort_ref, unsort_ref, pick_ref, cot_out_ref):
    me = me_ref[0]
    groups, tokens = owner_ref.shape[1:]
    rows = sort_ref.shape[0]
    slots = 2 * (tokens // block)
    owner = [owner_ref[k] for k in range(2)]
    pos = [pos_ref[k] for k in range(2)]
    cot = [cot_ref[k].astype(F32) for k in range(2)]
    token = lax.broadcasted_iota(jnp.int32, (groups, tokens), 1)
    in_block = token % block
    rank = [jnp.zeros((groups, tokens), jnp.int32), (owner[0] == owner[1]).astype(jnp.int32)]
    for shift in range(1, block):
        for other in range(2):
            moved = pltpu.roll(owner[other], shift, 1)
            for k in range(2):
                hit = (moved == owner[k]) & (in_block >= shift)
                rank[k] = rank[k] + hit.astype(jnp.int32)
    place = [2 * (token // block) + rank[k] for k in range(2)]
    held = [pos[k] >= 0 for k in range(2)]

    mine = lax.broadcasted_iota(jnp.int32, (groups, tokens), 0) == me
    slot_row = lax.broadcasted_iota(jnp.int32, (groups * slots, tokens), 0)
    for k in range(2):
        key = jnp.where(held[k], owner[k] * slots + place[k], -1)
        key = jnp.sum(jnp.where(mine, key, 0), axis=0, keepdims=True)
        pick_ref[k] = jnp.where(slot_row == key, 1.0, 0.0).astype(BF16)

    received = [jnp.where(held[k] & (owner[k] == me), place[k], -1) for k in range(2)]
    high = [((pos[k] + 1) // 32).astype(F32).astype(BF16) for k in range(2)]
    low = [((pos[k] + 1) % 32).astype(F32).astype(BF16) for k in range(2)]
    cot = [cot[k].astype(BF16) for k in range(2)]
    pair = 128 // slots
    cot_total = jnp.zeros((rows, 128), F32)
    lane_row = lax.broadcasted_iota(jnp.int32, (128, tokens), 0)
    buffer_row = lax.broadcasted_iota(jnp.int32, (rows, 128), 0)
    buffer_lane = lax.broadcasted_iota(jnp.int32, (128, rows), 1)
    for step in range(groups // pair):
        ones, highs, lows, cots = [], [], [], []
        for part in range(pair):
            g = step * pair + part
            for k in range(2):
                row = received[k][g : g + 1]
                row = jnp.where(row >= 0, row + part * slots, -1)
                ones.append(jnp.where(lane_row == row, 1.0, 0.0).astype(BF16))
                highs.append(high[k][g : g + 1])
                lows.append(low[k][g : g + 1])
                cots.append(cot[k][g : g + 1])
        chosen = jnp.concatenate(ones, axis=1)
        wide = chosen.shape[1]
        high_row = jnp.broadcast_to(jnp.concatenate(highs, axis=1), (128, wide))
        low_row = jnp.broadcast_to(jnp.concatenate(lows, axis=1), (128, wide))
        cot_row = jnp.broadcast_to(jnp.concatenate(cots, axis=1), (128, wide))
        at_lane = (mm(high_row, chosen, NT) * 32.0 + mm(low_row, chosen, NT)).astype(jnp.int32) - 1
        at_row = (mm(chosen, high_row, NT) * 32.0 + mm(chosen, low_row, NT)).astype(jnp.int32) - 1
        cot_lane = mm(cot_row, chosen, NT).astype(BF16)
        hit = jnp.where(buffer_row == at_lane[0:1], 1.0, 0.0).astype(BF16)
        sort_ref[:, step * 128 : (step + 1) * 128] = hit
        cot_total = cot_total + mm(hit, cot_lane, NT)
        at_row = jnp.concatenate([at_row] * (rows // 128), axis=1)
        unsort_ref[step * 128 : (step + 1) * 128, :] = jnp.where(buffer_lane == at_row, 1.0, 0.0).astype(BF16)
    cot_out_ref[...] = cot_total


def tables(block, rows, me, owner, pos, cot):
    groups, tokens = owner.shape[1:]
    received = groups * 2 * (tokens // block)
    vmem = pl.BlockSpec(memory_space=pltpu.VMEM)
    return pl.pallas_call(
        functools.partial(tables_kernel, block),
        out_shape=(
            jax.ShapeDtypeStruct((rows, received), BF16),
            jax.ShapeDtypeStruct((received, rows), BF16),
            jax.ShapeDtypeStruct((2, received, tokens), BF16),
            jax.ShapeDtypeStruct((rows, 128), F32),
        ),
        in_specs=[pl.BlockSpec(memory_space=pltpu.SMEM), vmem, vmem, vmem],
        out_specs=(vmem, vmem, vmem, vmem),
        compiler_params=pltpu.CompilerParams(vmem_limit_bytes=16 * 2**20),
        cost_estimate=pl.CostEstimate(flops=10**9, bytes_accessed=6 * 2**20, transcendentals=0),
    )(me, owner, pos, cot)


def started(pairs, sems):
    copies = []
    for n, (source, target) in enumerate(pairs):
        copies.append(pltpu.make_async_copy(source, target, sems.at[n]))
        copies[-1].start()
    return copies


def forward_kernel(
    sort_hbm, got_ref, weight_hbm, rows_hbm, part_ref, attn_hbm,
    sort, weight, rows, attn, sort_sems, weight_sems, rows_sems, attn_sem,
):
    groups, height, features = got_ref.shape
    adapters = weight.shape[0]
    capacity = sort.shape[0] // adapters
    slots = sort.shape[1] // groups
    at = [pl.ds(a * capacity, capacity) for a in range(adapters)]
    sort_in = started([(sort_hbm.at[i], sort.at[i]) for i in at], sort_sems)
    weight_in = started([(weight_hbm.at[a], weight.at[a]) for a in range(adapters)], weight_sems)
    block = attn.shape[1]
    attn[:, :, :features] = got_ref[:, slots : slots + block]
    attn[:, :, features:] = got_ref[:, slots + block :]
    out = started([(attn, attn_hbm)], attn_sem)
    got = got_ref[:, :slots].reshape(groups * slots, features)
    for a in range(adapters):
        sort_in[a].wait()
        rows[at[a]] = mm(sort[at[a]], got).astype(BF16)
        copy = pltpu.make_async_copy(rows.at[at[a]], rows_hbm.at[at[a]], rows_sems.at[a])
        copy.start()
        out.append(copy)
        weight_in[a].wait()
        part_ref[at[a]] = mm(rows[at[a]], weight[a]).astype(BF16)
    for copy in out:
        copy.wait()


ANYWHERE = pl.BlockSpec(memory_space=pl.ANY)
IN_VMEM = pl.BlockSpec(memory_space=pltpu.VMEM)


def forward(sort, got, weight):
    adapters, features, hidden = weight.shape
    rows, received = sort.shape
    slots = received // got.shape[0]
    attn = (got.shape[0], (got.shape[1] - slots) // 2, 2 * features)
    return pl.pallas_call(
        forward_kernel,
        out_shape=(
            jax.ShapeDtypeStruct((rows, features), BF16),
            jax.ShapeDtypeStruct((rows, hidden), BF16),
            jax.ShapeDtypeStruct(attn, BF16),
        ),
        in_specs=[ANYWHERE, IN_VMEM, ANYWHERE],
        out_specs=(ANYWHERE, IN_VMEM, ANYWHERE),
        scratch_shapes=[
            pltpu.VMEM(sort.shape, BF16),
            pltpu.VMEM(weight.shape, BF16),
            pltpu.VMEM((rows, features), BF16),
            pltpu.VMEM(attn, BF16),
            pltpu.SemaphoreType.DMA((adapters,)),
            pltpu.SemaphoreType.DMA((adapters,)),
            pltpu.SemaphoreType.DMA((adapters,)),
            pltpu.SemaphoreType.DMA((1,)),
        ],
        compiler_params=pltpu.CompilerParams(vmem_limit_bytes=58 * 2**20),
        cost_estimate=pl.CostEstimate(flops=10**9, bytes_accessed=6 * 2**20, transcendentals=0),
    )(sort, got, weight)


def backward_kernel(
    pre_ref, bias_ref, out_ref, cot_hbm, weight_hbm, unsort_hbm,
    half_hbm, bias_grad_ref, out_grad_ref, back_ref, reward_ref,
    cot_rows, weight, unsort, halves, grads, cot_sems, weight_sems, unsort_sems, half_sems,
):
    adapters, features, hidden = weight.shape
    capacity = pre_ref.shape[0] // adapters
    at = [pl.ds(a * capacity, capacity) for a in range(adapters)]
    (cot_in,) = started([(cot_hbm, cot_rows)], cot_sems)
    weight_in = started([(weight_hbm.at[a], weight.at[a]) for a in range(adapters)], weight_sems)
    (unsort_in,) = started([(unsort_hbm, unsort)], unsort_sems)
    out = []
    cot_in.wait()
    for a in range(adapters):
        read_out = out_ref[a : a + 1]
        pre = pre_ref[at[a]].astype(F32) + bias_ref[a : a + 1]
        s = 1.0 / (1.0 + jnp.exp(-pre))
        cot = jnp.concatenate([cot_rows[at[a]]] * (hidden // 128), axis=1)
        activated = pre * s
        grad_pre = cot * read_out * s * (1.0 + pre * (1.0 - s))
        halves[at[a]] = grad_pre.astype(BF16)
        copy = pltpu.make_async_copy(halves.at[at[a]], half_hbm.at[at[a]], half_sems.at[a])
        copy.start()
        out.append(copy)
        bias_grad_ref[a : a + 1] = jnp.sum(grad_pre, axis=0, keepdims=True)
        out_grad_ref[a : a + 1] = jnp.sum(cot * activated, axis=0, keepdims=True)
        reward = jnp.sum(activated * read_out, axis=1, keepdims=True)
        grads[at[a], features:] = jnp.broadcast_to(reward, (capacity, 128)).astype(BF16)
        weight_in[a].wait()
        grads[at[a], :features] = mm(halves[at[a]], weight[a], NT).astype(BF16)
    unsort_in.wait()
    back = mm(unsort[...], grads[...]).astype(BF16)
    back_ref[...] = back[:, :features]
    first = lax.broadcasted_iota(jnp.int32, (16, 128), 1) == 0
    first = jnp.where(first, 1.0, 0.0).astype(BF16)
    reward_ref[...] = mm(first, back[:, features:], NT).astype(BF16)
    for copy in out:
        copy.wait()


def backward(pre, bias, read_out, cot, weight, unsort):
    adapters, features, hidden = weight.shape
    received, rows = unsort.shape
    return pl.pallas_call(
        backward_kernel,
        out_shape=(
            jax.ShapeDtypeStruct((rows, hidden), BF16),
            jax.ShapeDtypeStruct((adapters, hidden), F32),
            jax.ShapeDtypeStruct((adapters, hidden), F32),
            jax.ShapeDtypeStruct((received, features), BF16),
            jax.ShapeDtypeStruct((16, received), BF16),
        ),
        in_specs=[IN_VMEM, IN_VMEM, IN_VMEM, ANYWHERE, ANYWHERE, ANYWHERE],
        out_specs=(ANYWHERE, IN_VMEM, IN_VMEM, IN_VMEM, IN_VMEM),
        scratch_shapes=[
            pltpu.VMEM(cot.shape, F32),
            pltpu.VMEM(weight.shape, BF16),
            pltpu.VMEM(unsort.shape, BF16),
            pltpu.VMEM((rows, hidden), BF16),
            pltpu.VMEM((rows, features + 128), BF16),
            pltpu.SemaphoreType.DMA((1,)),
            pltpu.SemaphoreType.DMA((adapters,)),
            pltpu.SemaphoreType.DMA((1,)),
            pltpu.SemaphoreType.DMA((adapters,)),
        ],
        compiler_params=pltpu.CompilerParams(vmem_limit_bytes=58 * 2**20),
        cost_estimate=pl.CostEstimate(flops=10**9, bytes_accessed=8 * 2**20, transcendentals=2**19),
    )(pre, bias, read_out, cot, weight, unsort)


def pick_kernel(pick_ref, group_ref, attn_ref, out_ref):
    owners, height, features = out_ref.shape
    block = attn_ref.shape[0]
    slots = height - 2 * block
    chosen = pick_ref[0] + pick_ref[1]
    out = mm(chosen, group_ref[...]).astype(BF16)
    out_ref[:, :slots] = out.reshape(owners, slots, features)
    for o in range(owners):
        start = 2 * o * features
        left = attn_ref[:, start : start + features]
        right = attn_ref[:, start + features : start + 2 * features]
        out_ref[o, slots:] = jnp.concatenate([left, right], axis=0)


def call(kernel, outs, mflops, mbytes, *args):
    vmem = pl.BlockSpec(memory_space=pltpu.VMEM)
    smem = pl.BlockSpec(memory_space=pltpu.SMEM)
    return pl.pallas_call(
        kernel,
        out_shape=tuple(jax.ShapeDtypeStruct(shape, dtype) for shape, dtype in outs),
        in_specs=[smem if arg.ndim == 1 else vmem for arg in args],
        out_specs=tuple(vmem for _ in outs),
        compiler_params=pltpu.CompilerParams(vmem_limit_bytes=12 * 2**20),
        cost_estimate=pl.CostEstimate(
            flops=mflops * 10**6, bytes_accessed=mbytes * 2**20, transcendentals=0
        ),
    )(*args)


def local(
    hidden_states, attn_input, rule_ids, slot_ids, cotangent, adapter_in, adapter_bias, adapter_out
):
    dp_size = lax.axis_size("dp")
    rule_size = lax.axis_size("rule")
    block = hidden_states.shape[0]
    adapters, feature_cols, hidden_units = adapter_in.shape
    tokens = block * rule_size
    capacity = 4 * block * rule_size // adapters
    rows = adapters * capacity
    slots = 2 * rule_size

    group_rows = lax.all_to_all(hidden_states, "rule", split_axis=1, concat_axis=0, tiled=True)

    rule_all = rule_ids.T.reshape(2, dp_size, tokens)
    slot_all = slot_ids.T.reshape(2, dp_size, tokens)
    cot_all = cotangent.T.reshape(2, dp_size, tokens)
    owner = rule_all // adapters
    pos = jnp.where(slot_all >= 0, rule_all % adapters * capacity + slot_all, -1)
    me = lax.axis_index("dp").astype(jnp.int32).reshape(1)
    sort, unsort, pick, cot_rows = tables(block, rows, me, owner, pos, cot_all)
    (outgoing,) = call(
        pick_kernel, [((dp_size, slots + 2 * block, feature_cols), BF16)], 200, 2,
        pick, group_rows, attn_input,
    )
    got = lax.all_to_all(outgoing, "dp", split_axis=0, concat_axis=0, tiled=True)
    rows_buf, partial_pre, attn_cols = forward(sort, got, adapter_in)
    attn_all = lax.all_gather(attn_cols, "rule", axis=1, tiled=True)
    shares = lax.all_to_all(partial_pre, "rule", split_axis=0, concat_axis=0, tiled=True)
    share = jnp.sum(
        shares.reshape(rule_size, rows // rule_size, hidden_units).astype(F32), axis=0
    ).astype(BF16)
    share = jnp.broadcast_to(share[None], (rule_size,) + share.shape).reshape(rows, hidden_units)
    preact = lax.all_to_all(share, "rule", split_axis=0, concat_axis=0, tiled=True)

    grad_half, bias_grad, out_grad, back, reward = backward(
        preact, adapter_bias, adapter_out, cot_rows, adapter_in, unsort
    )
    returned = lax.all_to_all(back, "dp", split_axis=0, concat_axis=0, tiled=True)
    state_grad = mm(pick[0] + pick[1], returned, TN).astype(BF16)
    attn_all, state_grad = lax.optimization_barrier((attn_all, state_grad))
    cut = tokens // 2 - 8
    width = attn_all.shape[2]
    attn_low = attn_all[:, :cut].reshape(dp_size * cut, width)
    attn_high = attn_all[:, cut:].reshape(dp_size * (tokens - cut), width)
    state_low = lax.all_gather(state_grad[:cut], "dp", axis=0, tiled=True)
    state_high = lax.all_gather(state_grad[cut:], "dp", axis=0, tiled=True)

    reward_back = lax.all_to_all(
        reward[0].reshape(dp_size, slots), "dp", split_axis=0, concat_axis=0, tiled=True
    )
    rewards = lax.dot_general(
        pick, reward_back.reshape(-1), (((1,), (0,)), ((), ())), preferred_element_type=F32
    )
    rewards = rewards.astype(BF16).T
    in_grad = jnp.einsum(
        "acd,acr->adr",
        rows_buf.reshape(adapters, capacity, feature_cols),
        grad_half.reshape(adapters, capacity, hidden_units),
        preferred_element_type=F32,
    ).astype(BF16)
    o_proj_grad = mm(state_low, attn_low, TN) + mm(state_high, attn_high, TN)
    o_proj_grad = o_proj_grad.astype(BF16)
    return (rewards, in_grad, bias_grad, out_grad, o_proj_grad)


def solution(mesh):
    placed = (
        P(("dp", "rule"), None),
        P(("dp", "rule"), None),
        P(),
        P(),
        P(),
        P("dp", "rule", None),
        P("dp", None),
        P("dp", None),
    )
    return jax.shard_map(
        local,
        mesh=mesh,
        in_specs=placed,
        out_specs=(
            P("dp", None),
            P("dp", "rule", None),
            P("dp", None),
            P("dp", None),
            P("rule", "dp"),
        ),
        check_vma=False,
    )
```

```python
import functools

import jax
import jax.numpy as jnp
from jax import lax
from jax.experimental import pallas as pl
from jax.experimental.pallas import tpu as pltpu
from jax.sharding import PartitionSpec as P

BF16 = jnp.bfloat16
F32 = jnp.float32
NN = (((1,), (0,)), ((), ()))
NT = (((1,), (1,)), ((), ()))
TN = (((0,), (0,)), ((), ()))


def mm(a, b, dims=NN):
    return lax.dot_general(a, b, dims, preferred_element_type=F32)


def select_kernel(adapters, rule_ref, slot_ref, hidden_ref, attn_ref, rows_ref, attn_out_ref):
    slices, owners, width = rows_ref.shape
    features = width // 2
    block = hidden_ref.shape[0]
    pairs = [(t, k) for t in range(block) for k in range(2)]
    owner = [rule_ref[k, t] // adapters for t, k in pairs]
    row = lax.broadcasted_iota(jnp.int32, (2 * owners, block), 0)
    token = lax.broadcasted_iota(jnp.int32, (2 * owners, block), 1)
    chosen = jnp.zeros((2 * owners, block), F32)
    for n, (t, k) in enumerate(pairs):
        rank = jnp.int32(0)
        for m in range(n):
            rank = rank + jnp.where(owner[m] == owner[n], 1, 0)
        key = jnp.where(slot_ref[k, t] >= 0, rank * owners + owner[n], -1)
        chosen = chosen + jnp.where((row == key) & (token == t), 1.0, 0.0)
    chosen = chosen.astype(BF16)
    for f in range(slices):
        out = mm(chosen, hidden_ref[:, f * features : (f + 1) * features]).astype(BF16)
        rows_ref[f, :, :features] = out[:owners]
        rows_ref[f, :, features:] = out[owners:]
    piece = attn_out_ref.shape[2]
    parts = slices // block
    for o in range(owners):
        for c in range(parts):
            start = (o * parts + c) * piece
            attn_out_ref[o, c * block : (c + 1) * block] = attn_ref[:, start : start + piece]


def tables_kernel(
    block, me_ref, owner_ref, pos_ref, cot_ref, lane_ref, row_ref, pick_ref, moved_ref, cot_out_ref
):
    me = me_ref[0]
    groups, tokens = owner_ref.shape[1:]
    rows = cot_out_ref.shape[0]
    blocks = tokens // block
    slots = 2 * blocks
    owner = [owner_ref[k] for k in range(2)]
    pos = [pos_ref[k] for k in range(2)]
    token = lax.broadcasted_iota(jnp.int32, (groups, tokens), 1)
    in_block = token % block
    rank = [jnp.zeros((groups, tokens), jnp.int32), (owner[0] == owner[1]).astype(jnp.int32)]
    for shift in range(1, block):
        for other in range(2):
            moved = pltpu.roll(owner[other], shift, 1)
            for k in range(2):
                hit = (moved == owner[k]) & (in_block >= shift)
                rank[k] = rank[k] + hit.astype(jnp.int32)
    place = [rank[k] * blocks + token // block for k in range(2)]
    held = [pos[k] >= 0 for k in range(2)]

    mine = lax.broadcasted_iota(jnp.int32, (groups, tokens), 0) == me
    slot_row = lax.broadcasted_iota(jnp.int32, (groups * slots, tokens), 0)
    total = jnp.zeros((groups * slots, tokens), F32)
    for k in range(2):
        key = jnp.where(held[k], owner[k] * slots + place[k], -1)
        key = jnp.sum(jnp.where(mine, key, 0), axis=0, keepdims=True)
        pick = jnp.where(slot_row == key, 1.0, 0.0)
        total = total + pick
        pick_ref[k] = pick.astype(BF16)
    before = lax.broadcasted_iota(jnp.int32, (tokens, tokens), 0)
    after = lax.broadcasted_iota(jnp.int32, (tokens, tokens), 1)
    order = jnp.where(before % block * blocks + before // block == after, 1.0, 0.0).astype(BF16)
    moved_ref[...] = mm(total.astype(BF16), order).astype(BF16)

    received = [jnp.where(held[k] & (owner[k] == me), place[k], -1) for k in range(2)]
    high = [((pos[k] + 1) // 32).astype(F32).astype(BF16) for k in range(2)]
    low = [((pos[k] + 1) % 32).astype(F32).astype(BF16) for k in range(2)]
    cot = [cot_ref[k] for k in range(2)]
    batch = 128 // blocks
    steps = groups // batch
    cot_total = jnp.zeros((rows, 128), F32)
    lane_row = lax.broadcasted_iota(jnp.int32, (128, tokens), 0)
    buffer_row = lax.broadcasted_iota(jnp.int32, (rows, 128), 0)
    for r in range(2):
        for step in range(steps):
            ones, highs, lows, cots = [], [], [], []
            for part in range(batch):
                g = step * batch + part
                for k in range(2):
                    row = received[k][g : g + 1] - r * blocks
                    row = jnp.where((row >= 0) & (row < blocks), row + part * blocks, -1)
                    ones.append(jnp.where(lane_row == row, 1.0, 0.0).astype(BF16))
                    highs.append(high[k][g : g + 1])
                    lows.append(low[k][g : g + 1])
                    cots.append(cot[k][g : g + 1])
            chosen = jnp.concatenate(ones, axis=1)
            wide = chosen.shape[1]
            high_row = jnp.broadcast_to(jnp.concatenate(highs, axis=1), (128, wide))
            low_row = jnp.broadcast_to(jnp.concatenate(lows, axis=1), (128, wide))
            cot_row = jnp.broadcast_to(jnp.concatenate(cots, axis=1), (128, wide))
            at_lane = mm(high_row, chosen, NT) * 32.0 + mm(low_row, chosen, NT)
            at_lane = at_lane.astype(jnp.int32) - 1
            at_row = mm(chosen, high_row, NT) * 32.0 + mm(chosen, low_row, NT)
            at_row = at_row.astype(jnp.int32) - 1
            cot_lane = mm(cot_row, chosen, NT).astype(BF16)
            hit = jnp.where(buffer_row == at_lane[0:1], 1.0, 0.0).astype(BF16)
            cot_total = cot_total + mm(hit, cot_lane, NT)
            lane = (r * steps + step) * 128
            lane_ref[:, lane : lane + 128] = at_lane[0:8]
            for part in range(batch):
                at = (step * batch + part) * slots + r * blocks
                row_ref[at : at + blocks] = at_row[part * blocks : (part + 1) * blocks]
    cot_out_ref[...] = cot_total


def started(pairs, sems):
    copies = []
    for n, (source, target) in enumerate(pairs):
        copies.append(pltpu.make_async_copy(source, target, sems.at[n]))
        copies[-1].start()
    return copies


def forward_kernel(
    lane_ref, got_ref, weight_hbm, rows_hbm, part_ref, attn_hbm,
    weight, rows, attn, weight_sems, rows_sem, attn_sem,
):
    adapters, features, hidden = weight.shape
    capacity = rows.shape[0] // adapters
    blocks = got_ref.shape[0]
    weight_in = started([(weight_hbm.at[a], weight.at[a]) for a in range(adapters)], weight_sems)
    attn[...] = got_ref[:, 2 * features :]
    (attn_out,) = started([(attn, attn_hbm)], attn_sem)
    buffer_row = lax.broadcasted_iota(jnp.int32, (rows.shape[0], blocks), 0)
    total = jnp.zeros(rows.shape, F32)
    for r in range(2):
        hit = buffer_row == lane_ref[0:1, r * blocks : (r + 1) * blocks]
        hit = jnp.where(hit, 1.0, 0.0).astype(BF16)
        total = total + mm(hit, got_ref[:, r * features : (r + 1) * features])
    rows[...] = total.astype(BF16)
    (rows_out,) = started([(rows, rows_hbm)], rows_sem)
    for a in range(adapters):
        weight_in[a].wait()
        at = slice(a * capacity, (a + 1) * capacity)
        part_ref[at] = mm(rows[at], weight[a]).astype(BF16)
    attn_out.wait()
    rows_out.wait()


ANYWHERE = pl.BlockSpec(memory_space=pl.ANY)
IN_VMEM = pl.BlockSpec(memory_space=pltpu.VMEM)


def forward(lane, got, weight):
    adapters, features, hidden = weight.shape
    rows = lane.shape[1]
    attn = (got.shape[0], got.shape[1] - 2 * features)
    return pl.pallas_call(
        forward_kernel,
        out_shape=(
            jax.ShapeDtypeStruct((rows, features), BF16),
            jax.ShapeDtypeStruct((rows, hidden), BF16),
            jax.ShapeDtypeStruct(attn, BF16),
        ),
        in_specs=[IN_VMEM, IN_VMEM, ANYWHERE],
        out_specs=(ANYWHERE, IN_VMEM, ANYWHERE),
        scratch_shapes=[
            pltpu.VMEM(weight.shape, BF16),
            pltpu.VMEM((rows, features), BF16),
            pltpu.VMEM(attn, BF16),
            pltpu.SemaphoreType.DMA((adapters,)),
            pltpu.SemaphoreType.DMA((1,)),
            pltpu.SemaphoreType.DMA((1,)),
        ],
        compiler_params=pltpu.CompilerParams(vmem_limit_bytes=56 * 2**20),
        cost_estimate=pl.CostEstimate(flops=10**9, bytes_accessed=6 * 2**20, transcendentals=0),
    )(lane, got, weight)


def backward_kernel(
    pre_ref, bias_ref, out_ref, cot_hbm, weight_hbm, row_hbm,
    half_hbm, bias_grad_ref, out_grad_ref, back_ref, reward_ref,
    cot_rows, weight, unsort, row, halves, grads, cot_sems, weight_sems, row_sems, half_sems,
):
    adapters, features, hidden = weight.shape
    capacity = pre_ref.shape[0] // adapters
    at = [pl.ds(a * capacity, capacity) for a in range(adapters)]
    (cot_in,) = started([(cot_hbm, cot_rows)], cot_sems)
    weight_in = started([(weight_hbm.at[a], weight.at[a]) for a in range(adapters)], weight_sems)
    (row_in,) = started([(row_hbm, row)], row_sems)
    out = []
    cot_in.wait()
    row_in.wait()
    lane = lax.broadcasted_iota(jnp.int32, (capacity, 128), 1)
    for a in range(adapters):
        for n in range(0, unsort.shape[1], 128):
            hit = row[at[a]] - n == lane
            unsort[at[a], n : n + 128] = jnp.where(hit, 1.0, 0.0).astype(BF16)
    for a in range(adapters):
        read_out = out_ref[a : a + 1]
        pre = pre_ref[at[a]].astype(F32) + bias_ref[a : a + 1]
        s = 1.0 / (1.0 + jnp.exp(-pre))
        cot = jnp.concatenate([cot_rows[at[a]]] * (hidden // 128), axis=1)
        activated = pre * s
        grad_pre = cot * read_out * s * (1.0 + pre * (1.0 - s))
        halves[at[a]] = grad_pre.astype(BF16)
        copy = pltpu.make_async_copy(halves.at[at[a]], half_hbm.at[at[a]], half_sems.at[a])
        copy.start()
        out.append(copy)
        bias_grad_ref[a : a + 1] = jnp.sum(grad_pre, axis=0, keepdims=True)
        out_grad_ref[a : a + 1] = jnp.sum(cot * activated, axis=0, keepdims=True)
        reward = jnp.sum(activated * read_out, axis=1, keepdims=True)
        grads[at[a], features:] = jnp.broadcast_to(reward, (capacity, 128)).astype(BF16)
        weight_in[a].wait()
        grads[at[a], :features] = mm(halves[at[a]], weight[a], NT).astype(BF16)
    back = mm(unsort[...], grads[...]).astype(BF16)
    back_ref[...] = back[:, :features]
    first = lax.broadcasted_iota(jnp.int32, (16, 128), 1) == 0
    first = jnp.where(first, 1.0, 0.0).astype(BF16)
    reward_ref[...] = mm(first, back[:, features:], NT).astype(BF16)
    for copy in out:
        copy.wait()


def backward(pre, bias, read_out, cot, weight, row):
    adapters, features, hidden = weight.shape
    received, rows = row.shape[0], pre.shape[0]
    return pl.pallas_call(
        backward_kernel,
        out_shape=(
            jax.ShapeDtypeStruct((rows, hidden), BF16),
            jax.ShapeDtypeStruct((adapters, hidden), F32),
            jax.ShapeDtypeStruct((adapters, hidden), F32),
            jax.ShapeDtypeStruct((received, features), BF16),
            jax.ShapeDtypeStruct((16, received), BF16),
        ),
        in_specs=[IN_VMEM, IN_VMEM, IN_VMEM, ANYWHERE, ANYWHERE, ANYWHERE],
        out_specs=(ANYWHERE, IN_VMEM, IN_VMEM, IN_VMEM, IN_VMEM),
        scratch_shapes=[
            pltpu.VMEM(cot.shape, F32),
            pltpu.VMEM(weight.shape, BF16),
            pltpu.VMEM((received, rows), BF16),
            pltpu.VMEM(row.shape, jnp.int32),
            pltpu.VMEM((rows, hidden), BF16),
            pltpu.VMEM((rows, features + 128), BF16),
            pltpu.SemaphoreType.DMA((1,)),
            pltpu.SemaphoreType.DMA((adapters,)),
            pltpu.SemaphoreType.DMA((1,)),
            pltpu.SemaphoreType.DMA((adapters,)),
        ],
        compiler_params=pltpu.CompilerParams(vmem_limit_bytes=58 * 2**20),
        cost_estimate=pl.CostEstimate(flops=10**9, bytes_accessed=8 * 2**20, transcendentals=2**19),
    )(pre, bias, read_out, cot, weight, row)


def project_kernel(state_hbm, attn_ref, out_ref, state, sems):
    block, groups, blocks, features = state.shape
    parts = attn_ref.shape[0]
    state_in = started([(state_hbm.at[:, t], state.at[t]) for t in range(block)], sems)
    total = jnp.zeros(out_ref.shape, F32)
    for t in range(block):
        columns = jnp.concatenate([attn_ref[c, t] for c in range(parts)], axis=1)
        state_in[t].wait()
        total = total + mm(state[t].reshape(groups * blocks, features), columns, TN)
    out_ref[...] = total.astype(BF16)


def project(state, attn):
    groups, block, blocks, features = state.shape
    return pl.pallas_call(
        project_kernel,
        out_shape=jax.ShapeDtypeStruct((features, attn.shape[0] * attn.shape[3]), BF16),
        in_specs=[ANYWHERE, IN_VMEM],
        out_specs=IN_VMEM,
        scratch_shapes=[
            pltpu.VMEM((block, groups, blocks, features), BF16),
            pltpu.SemaphoreType.DMA((block,)),
        ],
        compiler_params=pltpu.CompilerParams(vmem_limit_bytes=52 * 2**20),
        cost_estimate=pl.CostEstimate(flops=10**9, bytes_accessed=6 * 2**20, transcendentals=0),
    )(state, attn)


def local(
    hidden_states, attn_input, rule_ids, slot_ids, cotangent, adapter_in, adapter_bias, adapter_out
):
    dp_size = lax.axis_size("dp")
    rule_size = lax.axis_size("rule")
    block = hidden_states.shape[0]
    adapters, feature_cols, hidden_units = adapter_in.shape
    tokens = block * rule_size
    capacity = 4 * block * rule_size // adapters
    rows = adapters * capacity
    slots = 2 * rule_size

    me = lax.axis_index("dp").astype(jnp.int32)
    first = (me * rule_size + lax.axis_index("rule").astype(jnp.int32)) * block
    rules, slot = rule_ids.T, slot_ids.T
    piece = 2 * feature_cols * block // rule_size
    select_out = (
        jax.ShapeDtypeStruct((rule_size, dp_size, 2 * feature_cols), BF16),
        jax.ShapeDtypeStruct((dp_size, rule_size, piece), BF16),
    )
    in_smem = pl.BlockSpec(memory_space=pltpu.SMEM)
    rows_out, attn_out = pl.pallas_call(
        functools.partial(select_kernel, adapters),
        out_shape=select_out,
        in_specs=[in_smem, in_smem, IN_VMEM, IN_VMEM],
        out_specs=(IN_VMEM, IN_VMEM),
        compiler_params=pltpu.CompilerParams(vmem_limit_bytes=8 * 2**20),
        cost_estimate=pl.CostEstimate(flops=10**8, bytes_accessed=2**20, transcendentals=0),
    )(
        lax.dynamic_slice(rules, (0, first), (2, block)),
        lax.dynamic_slice(slot, (0, first), (2, block)),
        hidden_states,
        attn_input,
    )
    outgoing = jnp.concatenate([jnp.swapaxes(rows_out, 0, 1), attn_out], axis=2)
    outgoing = outgoing.reshape(dp_size * rule_size, 2 * feature_cols + piece)
    got = lax.all_to_all(outgoing, ("dp", "rule"), split_axis=0, concat_axis=0, tiled=True)

    rule_all = rules.reshape(2, dp_size, tokens)
    slot_all = slot.reshape(2, dp_size, tokens)
    cot_all = cotangent.T.reshape(2, dp_size, tokens)
    owner = rule_all // adapters
    pos = jnp.where(slot_all >= 0, rule_all % adapters * capacity + slot_all, -1)
    received = dp_size * slots
    lane, row, pick, pick_moved, cot_rows = pl.pallas_call(
        functools.partial(tables_kernel, block),
        out_shape=(
            jax.ShapeDtypeStruct((8, received), jnp.int32),
            jax.ShapeDtypeStruct((received, 128), jnp.int32),
            jax.ShapeDtypeStruct((2, received, tokens), BF16),
            jax.ShapeDtypeStruct((received, tokens), BF16),
            jax.ShapeDtypeStruct((rows, 128), F32),
        ),
        in_specs=[in_smem, IN_VMEM, IN_VMEM, IN_VMEM],
        out_specs=(IN_VMEM,) * 5,
        compiler_params=pltpu.CompilerParams(vmem_limit_bytes=24 * 2**20),
        cost_estimate=pl.CostEstimate(flops=10**9, bytes_accessed=2**22, transcendentals=0),
    )(me.reshape(1), owner, pos, cot_all)

    rows_buf, partial_pre, attn_cols = forward(lane, got, adapter_in)
    attn_all = lax.all_gather(attn_cols, "rule", axis=0, tiled=True)
    attn_all = attn_all.reshape(rule_size // block, block, dp_size * rule_size, piece)
    shares = lax.all_to_all(partial_pre, "rule", split_axis=0, concat_axis=0, tiled=True)
    share = jnp.sum(
        shares.reshape(rule_size, rows // rule_size, hidden_units).astype(F32), axis=0
    ).astype(BF16)
    share = jnp.broadcast_to(share[None], (rule_size,) + share.shape).reshape(rows, hidden_units)
    preact = lax.all_to_all(share, "rule", split_axis=0, concat_axis=0, tiled=True)

    grad_half, bias_grad, out_grad, back, reward = backward(
        preact, adapter_bias, adapter_out, cot_rows, adapter_in, row
    )
    returned = lax.all_to_all(back, "dp", split_axis=0, concat_axis=0, tiled=True)
    state_grad = mm(pick_moved, returned, TN).astype(BF16)
    attn_all, state_grad = lax.optimization_barrier((attn_all, state_grad))
    state_all = lax.all_gather(state_grad, "dp", axis=0, tiled=True)
    state_all = state_all.reshape(dp_size, block, rule_size, feature_cols)

    reward_back = lax.all_to_all(
        reward[0].reshape(dp_size, slots), "dp", split_axis=0, concat_axis=0, tiled=True
    )
    rewards = lax.dot_general(
        pick, reward_back.reshape(-1), (((1,), (0,)), ((), ())), preferred_element_type=F32
    )
    rewards = rewards.astype(BF16).T
    in_grad = jnp.einsum(
        "acd,acr->adr",
        rows_buf.reshape(adapters, capacity, feature_cols),
        grad_half.reshape(adapters, capacity, hidden_units),
        preferred_element_type=F32,
    ).astype(BF16)
    o_proj_grad = project(state_all, attn_all)
    return (rewards, in_grad, bias_grad, out_grad, o_proj_grad)


def solution(mesh):
    placed = (
        P(("dp", "rule"), None),
        P(("dp", "rule"), None),
        P(),
        P(),
        P(),
        P("dp", "rule", None),
        P("dp", None),
        P("dp", None),
    )
    return jax.shard_map(
        local,
        mesh=mesh,
        in_specs=placed,
        out_specs=(
            P("dp", None),
            P("dp", "rule", None),
            P("dp", None),
            P("dp", None),
            P("rule", "dp"),
        ),
        check_vma=False,
    )
```

```python
import functools

import jax
import jax.numpy as jnp
from jax import lax
from jax.experimental import pallas as pl
from jax.experimental.pallas import tpu as pltpu
from jax.sharding import PartitionSpec as P

BF16 = jnp.bfloat16
F32 = jnp.float32
NN = (((1,), (0,)), ((), ()))
NT = (((1,), (1,)), ((), ()))
TN = (((0,), (0,)), ((), ()))


def mm(a, b, dims=NN):
    return lax.dot_general(a, b, dims, preferred_element_type=F32)


def tables_kernel(block, me_ref, owner_ref, pos_ref, cot_ref, lane_ref, row_ref, pick_ref, cot_out_ref):
    me = me_ref[0]
    groups, tokens = owner_ref.shape[1:]
    rows = cot_out_ref.shape[0]
    slots = 2 * (tokens // block)
    owner = [owner_ref[k] for k in range(2)]
    pos = [pos_ref[k] for k in range(2)]
    cot = [cot_ref[k].astype(F32) for k in range(2)]
    token = lax.broadcasted_iota(jnp.int32, (groups, tokens), 1)
    in_block = token % block
    rank = [jnp.zeros((groups, tokens), jnp.int32), (owner[0] == owner[1]).astype(jnp.int32)]
    for shift in range(1, block):
        for other in range(2):
            moved = pltpu.roll(owner[other], shift, 1)
            for k in range(2):
                hit = (moved == owner[k]) & (in_block >= shift)
                rank[k] = rank[k] + hit.astype(jnp.int32)
    place = [2 * (token // block) + rank[k] for k in range(2)]
    held = [pos[k] >= 0 for k in range(2)]

    mine = lax.broadcasted_iota(jnp.int32, (groups, tokens), 0) == me
    slot_row = lax.broadcasted_iota(jnp.int32, (groups * slots, tokens), 0)
    for k in range(2):
        key = jnp.where(held[k], owner[k] * slots + place[k], -1)
        key = jnp.sum(jnp.where(mine, key, 0), axis=0, keepdims=True)
        pick_ref[k] = jnp.where(slot_row == key, 1.0, 0.0).astype(BF16)

    received = [jnp.where(held[k] & (owner[k] == me), place[k], -1) for k in range(2)]
    high = [((pos[k] + 1) // 32).astype(F32).astype(BF16) for k in range(2)]
    low = [((pos[k] + 1) % 32).astype(F32).astype(BF16) for k in range(2)]
    cot = [cot[k].astype(BF16) for k in range(2)]
    pair = 128 // slots
    cot_total = jnp.zeros((rows, 128), F32)
    lane_row = lax.broadcasted_iota(jnp.int32, (128, tokens), 0)
    buffer_row = lax.broadcasted_iota(jnp.int32, (rows, 128), 0)
    for step in range(groups // pair):
        ones, highs, lows, cots = [], [], [], []
        for part in range(pair):
            g = step * pair + part
            for k in range(2):
                row = received[k][g : g + 1]
                row = jnp.where(row >= 0, row + part * slots, -1)
                ones.append(jnp.where(lane_row == row, 1.0, 0.0).astype(BF16))
                highs.append(high[k][g : g + 1])
                lows.append(low[k][g : g + 1])
                cots.append(cot[k][g : g + 1])
        chosen = jnp.concatenate(ones, axis=1)
        wide = chosen.shape[1]
        high_row = jnp.broadcast_to(jnp.concatenate(highs, axis=1), (128, wide))
        low_row = jnp.broadcast_to(jnp.concatenate(lows, axis=1), (128, wide))
        cot_row = jnp.broadcast_to(jnp.concatenate(cots, axis=1), (128, wide))
        at_lane = (mm(high_row, chosen, NT) * 32.0 + mm(low_row, chosen, NT)).astype(jnp.int32) - 1
        at_row = (mm(chosen, high_row, NT) * 32.0 + mm(chosen, low_row, NT)).astype(jnp.int32) - 1
        cot_lane = mm(cot_row, chosen, NT).astype(BF16)
        hit = jnp.where(buffer_row == at_lane[0:1], 1.0, 0.0).astype(BF16)
        lane_ref[:, step * 128 : (step + 1) * 128] = at_lane[0:8]
        cot_total = cot_total + mm(hit, cot_lane, NT)
        row_ref[step * 128 : (step + 1) * 128, :] = at_row
    cot_out_ref[...] = cot_total


def tables(block, rows, me, owner, pos, cot):
    groups, tokens = owner.shape[1:]
    received = groups * 2 * (tokens // block)
    vmem = pl.BlockSpec(memory_space=pltpu.VMEM)
    return pl.pallas_call(
        functools.partial(tables_kernel, block),
        out_shape=(
            jax.ShapeDtypeStruct((8, received), jnp.int32),
            jax.ShapeDtypeStruct((received, 128), jnp.int32),
            jax.ShapeDtypeStruct((2, received, tokens), BF16),
            jax.ShapeDtypeStruct((rows, 128), F32),
        ),
        in_specs=[pl.BlockSpec(memory_space=pltpu.SMEM), vmem, vmem, vmem],
        out_specs=(vmem, vmem, vmem, vmem),
        compiler_params=pltpu.CompilerParams(vmem_limit_bytes=16 * 2**20),
        cost_estimate=pl.CostEstimate(flops=10**9, bytes_accessed=6 * 2**20, transcendentals=0),
    )(me, owner, pos, cot)


def forward_kernel(lane_ref, got_ref, weight_ref, rows_ref, part_ref, attn_ref, got):
    features = got.shape[1]
    capacity = rows_ref.shape[0]
    slots = got.shape[0] // got_ref.shape[0]
    block = attn_ref.shape[1]

    @pl.when(pl.program_id(0) == 0)
    def _():
        got[...] = got_ref[:, :slots].reshape(got.shape)
        attn_ref[:, :, :features] = got_ref[:, slots : slots + block]
        attn_ref[:, :, features:] = got_ref[:, slots + block :]

    row = lax.broadcasted_iota(jnp.int32, (capacity, got.shape[0]), 0)
    hit = row == lane_ref[0:1] - pl.program_id(0) * capacity
    rows = mm(jnp.where(hit, 1.0, 0.0).astype(BF16), got[...]).astype(BF16)
    rows_ref[...] = rows
    part_ref[...] = mm(rows, weight_ref[0]).astype(BF16)


def forward(lane, got, weight, rows):
    adapters, features, hidden = weight.shape
    received = lane.shape[1]
    capacity = rows // adapters
    slots = received // got.shape[0]
    attn = (got.shape[0], (got.shape[1] - slots) // 2, 2 * features)
    return pl.pallas_call(
        forward_kernel,
        grid=(adapters,),
        out_shape=(
            jax.ShapeDtypeStruct((rows, features), BF16),
            jax.ShapeDtypeStruct((rows, hidden), BF16),
            jax.ShapeDtypeStruct(attn, BF16),
        ),
        in_specs=[
            pl.BlockSpec((8, received), lambda a: (0, 0)),
            pl.BlockSpec(got.shape, lambda a: (0, 0, 0)),
            pl.BlockSpec((1, features, hidden), lambda a: (a, 0, 0)),
        ],
        out_specs=(
            pl.BlockSpec((capacity, features), lambda a: (a, 0)),
            pl.BlockSpec((capacity, hidden), lambda a: (a, 0)),
            pl.BlockSpec(attn, lambda a: (0, 0, 0)),
        ),
        scratch_shapes=[pltpu.VMEM((received, features), BF16)],
        compiler_params=pltpu.CompilerParams(vmem_limit_bytes=12 * 2**20),
        cost_estimate=pl.CostEstimate(flops=10**9, bytes_accessed=6 * 2**20, transcendentals=0),
    )(lane, got, weight)


def backward_kernel(
    pre_ref, bias_ref, out_ref, cot_ref, weight_ref, row_ref,
    half_ref, bias_grad_ref, out_grad_ref, back_ref, reward_ref, unsort, grads,
):
    a = pl.program_id(0)
    capacity, hidden = pre_ref.shape
    features = weight_ref.shape[1]
    read_out = out_ref[0]
    pre = pre_ref[...].astype(F32) + bias_ref[0]
    s = 1.0 / (1.0 + jnp.exp(-pre))
    cot = jnp.concatenate([cot_ref[...]] * (hidden // 128), axis=1)
    activated = pre * s
    grad_pre = cot * read_out * s * (1.0 + pre * (1.0 - s))
    half = grad_pre.astype(BF16)
    half_ref[...] = half
    bias_grad_ref[0] = jnp.sum(grad_pre, axis=0, keepdims=True)
    out_grad_ref[0] = jnp.sum(cot * activated, axis=0, keepdims=True)
    reward = jnp.sum(activated * read_out, axis=1, keepdims=True)
    at = pl.ds(pl.multiple_of(a * capacity, capacity), capacity)
    grads[at, :features] = mm(half, weight_ref[0], NT).astype(BF16)
    grads[at, features:] = jnp.broadcast_to(reward, (capacity, 128)).astype(BF16)

    height = row_ref.shape[0]
    part = pl.ds(pl.multiple_of(a * height, height), height)
    lane = lax.broadcasted_iota(jnp.int32, (height, 128), 1)
    for n in range(0, unsort.shape[1], 128):
        hit = row_ref[...] - n == lane
        unsort[part, n : n + 128] = jnp.where(hit, 1.0, 0.0).astype(BF16)

    @pl.when(a == pl.num_programs(0) - 1)
    def _():
        back = mm(unsort[...], grads[...]).astype(BF16)
        back_ref[...] = back[:, :features]
        first = lax.broadcasted_iota(jnp.int32, (16, 128), 1) == 0
        first = jnp.where(first, 1.0, 0.0).astype(BF16)
        reward_ref[...] = mm(first, back[:, features:], NT).astype(BF16)


def backward(pre, bias, read_out, cot, weight, row):
    adapters, features, hidden = weight.shape
    received, rows = row.shape[0], pre.shape[0]
    capacity = rows // adapters
    line = pl.BlockSpec((1, 1, hidden), lambda a: (a, 0, 0))
    half, bias_grad, out_grad, back, reward = pl.pallas_call(
        backward_kernel,
        grid=(adapters,),
        out_shape=(
            jax.ShapeDtypeStruct((rows, hidden), BF16),
            jax.ShapeDtypeStruct((adapters, 1, hidden), F32),
            jax.ShapeDtypeStruct((adapters, 1, hidden), F32),
            jax.ShapeDtypeStruct((received, features), BF16),
            jax.ShapeDtypeStruct((16, received), BF16),
        ),
        in_specs=[
            pl.BlockSpec((capacity, hidden), lambda a: (a, 0)),
            line,
            line,
            pl.BlockSpec((capacity, 128), lambda a: (a, 0)),
            pl.BlockSpec((1, features, hidden), lambda a: (a, 0, 0)),
            pl.BlockSpec((received // adapters, 128), lambda a: (a, 0)),
        ],
        out_specs=(
            pl.BlockSpec((capacity, hidden), lambda a: (a, 0)),
            line,
            line,
            pl.BlockSpec((received, features), lambda a: (0, 0)),
            pl.BlockSpec((16, received), lambda a: (0, 0)),
        ),
        scratch_shapes=[
            pltpu.VMEM((received, rows), BF16),
            pltpu.VMEM((rows, features + 128), BF16),
        ],
        compiler_params=pltpu.CompilerParams(vmem_limit_bytes=16 * 2**20),
        cost_estimate=pl.CostEstimate(flops=10**9, bytes_accessed=8 * 2**20, transcendentals=2**19),
    )(pre, bias[:, None], read_out[:, None], cot, weight, row)
    return half, bias_grad[:, 0], out_grad[:, 0], back, reward


def pick_kernel(pick_ref, group_ref, attn_ref, out_ref):
    owners, height, features = out_ref.shape
    block = attn_ref.shape[0]
    slots = height - 2 * block
    chosen = pick_ref[0] + pick_ref[1]
    out = mm(chosen, group_ref[...]).astype(BF16)
    out_ref[:, :slots] = out.reshape(owners, slots, features)
    for o in range(owners):
        start = 2 * o * features
        left = attn_ref[:, start : start + features]
        right = attn_ref[:, start + features : start + 2 * features]
        out_ref[o, slots:] = jnp.concatenate([left, right], axis=0)


def call(kernel, outs, mflops, mbytes, *args):
    vmem = pl.BlockSpec(memory_space=pltpu.VMEM)
    smem = pl.BlockSpec(memory_space=pltpu.SMEM)
    return pl.pallas_call(
        kernel,
        out_shape=tuple(jax.ShapeDtypeStruct(shape, dtype) for shape, dtype in outs),
        in_specs=[smem if arg.ndim == 1 else vmem for arg in args],
        out_specs=tuple(vmem for _ in outs),
        compiler_params=pltpu.CompilerParams(vmem_limit_bytes=12 * 2**20),
        cost_estimate=pl.CostEstimate(
            flops=mflops * 10**6, bytes_accessed=mbytes * 2**20, transcendentals=0
        ),
    )(*args)


def local(
    hidden_states, attn_input, rule_ids, slot_ids, cotangent, adapter_in, adapter_bias, adapter_out
):
    dp_size = lax.axis_size("dp")
    rule_size = lax.axis_size("rule")
    block = hidden_states.shape[0]
    adapters, feature_cols, hidden_units = adapter_in.shape
    tokens = block * rule_size
    capacity = 4 * block * rule_size // adapters
    rows = adapters * capacity
    slots = 2 * rule_size

    group_rows = lax.all_to_all(hidden_states, "rule", split_axis=1, concat_axis=0, tiled=True)

    rule_all = rule_ids.T.reshape(2, dp_size, tokens)
    slot_all = slot_ids.T.reshape(2, dp_size, tokens)
    cot_all = cotangent.T.reshape(2, dp_size, tokens)
    owner = rule_all // adapters
    pos = jnp.where(slot_all >= 0, rule_all % adapters * capacity + slot_all, -1)
    me = lax.axis_index("dp").astype(jnp.int32).reshape(1)
    lane, row, pick, cot_rows = tables(block, rows, me, owner, pos, cot_all)
    (outgoing,) = call(
        pick_kernel, [((dp_size, slots + 2 * block, feature_cols), BF16)], 200, 2,
        pick, group_rows, attn_input,
    )
    got = lax.all_to_all(outgoing, "dp", split_axis=0, concat_axis=0, tiled=True)
    rows_buf, partial_pre, attn_cols = forward(lane, got, adapter_in, rows)
    attn_all = lax.all_gather(attn_cols, "rule", axis=1, tiled=True)
    shares = lax.all_to_all(partial_pre, "rule", split_axis=0, concat_axis=0, tiled=True)
    share = jnp.sum(
        shares.reshape(rule_size, rows // rule_size, hidden_units).astype(F32), axis=0
    ).astype(BF16)
    share = jnp.broadcast_to(share[None], (rule_size,) + share.shape).reshape(rows, hidden_units)
    preact = lax.all_to_all(share, "rule", split_axis=0, concat_axis=0, tiled=True)

    grad_half, bias_grad, out_grad, back, reward = backward(
        preact, adapter_bias, adapter_out, cot_rows, adapter_in, row
    )
    returned = lax.all_to_all(back, "dp", split_axis=0, concat_axis=0, tiled=True)
    state_grad = mm(pick[0] + pick[1], returned, TN).astype(BF16)
    attn_all, state_grad = lax.optimization_barrier((attn_all, state_grad))
    cut = tokens // 2 - 8
    width = attn_all.shape[2]
    attn_low = attn_all[:, :cut].reshape(dp_size * cut, width)
    attn_high = attn_all[:, cut:].reshape(dp_size * (tokens - cut), width)
    state_low = lax.all_gather(state_grad[:cut], "dp", axis=0, tiled=True)
    state_high = lax.all_gather(state_grad[cut:], "dp", axis=0, tiled=True)

    reward_back = lax.all_to_all(
        reward[0].reshape(dp_size, slots), "dp", split_axis=0, concat_axis=0, tiled=True
    )
    rewards = lax.dot_general(
        pick, reward_back.reshape(-1), (((1,), (0,)), ((), ())), preferred_element_type=F32
    )
    rewards = rewards.astype(BF16).T
    in_grad = jnp.einsum(
        "acd,acr->adr",
        rows_buf.reshape(adapters, capacity, feature_cols),
        grad_half.reshape(adapters, capacity, hidden_units),
        preferred_element_type=F32,
    ).astype(BF16)
    o_proj_grad = mm(state_low, attn_low, TN) + mm(state_high, attn_high, TN)
    o_proj_grad = o_proj_grad.astype(BF16)
    return (rewards, in_grad, bias_grad, out_grad, o_proj_grad)


def solution(mesh):
    placed = (
        P(("dp", "rule"), None),
        P(("dp", "rule"), None),
        P(),
        P(),
        P(),
        P("dp", "rule", None),
        P("dp", None),
        P("dp", None),
    )
    return jax.shard_map(
        local,
        mesh=mesh,
        in_specs=placed,
        out_specs=(
            P("dp", None),
            P("dp", "rule", None),
            P("dp", None),
            P("dp", None),
            P("rule", "dp"),
        ),
        check_vma=False,
    )
```

```python
import functools

import jax
import jax.numpy as jnp
from jax import lax
from jax.experimental import pallas as pl
from jax.experimental.pallas import tpu as pltpu
from jax.sharding import PartitionSpec as P

BF16 = jnp.bfloat16
F32 = jnp.float32
NN = (((1,), (0,)), ((), ()))
NT = (((1,), (1,)), ((), ()))
TN = (((0,), (0,)), ((), ()))


def mm(a, b, dims=NN):
    return lax.dot_general(a, b, dims, preferred_element_type=F32)


def tables_kernel(block, me_ref, owner_ref, pos_ref, cot_ref, lane_ref, pick_ref, cot_out_ref):
    me = me_ref[0]
    groups, tokens = owner_ref.shape[1:]
    rows = cot_out_ref.shape[0]
    slots = 2 * (tokens // block)
    owner = [owner_ref[k] for k in range(2)]
    pos = [pos_ref[k] for k in range(2)]
    cot = [cot_ref[k].astype(F32) for k in range(2)]
    token = lax.broadcasted_iota(jnp.int32, (groups, tokens), 1)
    in_block = token % block
    rank = [jnp.zeros((groups, tokens), jnp.int32), (owner[0] == owner[1]).astype(jnp.int32)]
    for shift in range(1, block):
        for other in range(2):
            moved = pltpu.roll(owner[other], shift, 1)
            for k in range(2):
                hit = (moved == owner[k]) & (in_block >= shift)
                rank[k] = rank[k] + hit.astype(jnp.int32)
    place = [2 * (token // block) + rank[k] for k in range(2)]
    held = [pos[k] >= 0 for k in range(2)]

    mine = lax.broadcasted_iota(jnp.int32, (groups, tokens), 0) == me
    slot_row = lax.broadcasted_iota(jnp.int32, (groups * slots, tokens), 0)
    for k in range(2):
        key = jnp.where(held[k], owner[k] * slots + place[k], -1)
        key = jnp.sum(jnp.where(mine, key, 0), axis=0, keepdims=True)
        pick_ref[k] = jnp.where(slot_row == key, 1.0, 0.0).astype(BF16)

    received = [jnp.where(held[k] & (owner[k] == me), place[k], -1) for k in range(2)]
    high = [((pos[k] + 1) // 32).astype(F32).astype(BF16) for k in range(2)]
    low = [((pos[k] + 1) % 32).astype(F32).astype(BF16) for k in range(2)]
    cot = [cot[k].astype(BF16) for k in range(2)]
    pair = 128 // slots
    cot_total = jnp.zeros((rows, 128), F32)
    lane_row = lax.broadcasted_iota(jnp.int32, (128, tokens), 0)
    buffer_row = lax.broadcasted_iota(jnp.int32, (rows, 128), 0)
    for step in range(groups // pair):
        ones, highs, lows, cots = [], [], [], []
        for part in range(pair):
            g = step * pair + part
            for k in range(2):
                row = received[k][g : g + 1]
                row = jnp.where(row >= 0, row + part * slots, -1)
                ones.append(jnp.where(lane_row == row, 1.0, 0.0).astype(BF16))
                highs.append(high[k][g : g + 1])
                lows.append(low[k][g : g + 1])
                cots.append(cot[k][g : g + 1])
        chosen = jnp.concatenate(ones, axis=1)
        wide = chosen.shape[1]
        high_row = jnp.broadcast_to(jnp.concatenate(highs, axis=1), (128, wide))
        low_row = jnp.broadcast_to(jnp.concatenate(lows, axis=1), (128, wide))
        cot_row = jnp.broadcast_to(jnp.concatenate(cots, axis=1), (128, wide))
        at_lane = (mm(high_row, chosen, NT) * 32.0 + mm(low_row, chosen, NT)).astype(jnp.int32) - 1
        cot_lane = mm(cot_row, chosen, NT).astype(BF16)
        hit = jnp.where(buffer_row == at_lane[0:1], 1.0, 0.0).astype(BF16)
        lane_ref[:, step * 128 : (step + 1) * 128] = at_lane[0:8]
        cot_total = cot_total + mm(hit, cot_lane, NT)
    cot_out_ref[...] = cot_total.astype(BF16)


def tables(block, rows, me, owner, pos, cot):
    groups, tokens = owner.shape[1:]
    received = groups * 2 * (tokens // block)
    vmem = pl.BlockSpec(memory_space=pltpu.VMEM)
    return pl.pallas_call(
        functools.partial(tables_kernel, block),
        out_shape=(
            jax.ShapeDtypeStruct((8, received), jnp.int32),
            jax.ShapeDtypeStruct((2, received, tokens), BF16),
            jax.ShapeDtypeStruct((rows, 128), BF16),
        ),
        in_specs=[pl.BlockSpec(memory_space=pltpu.SMEM), vmem, vmem, vmem],
        out_specs=(vmem, vmem, vmem),
        compiler_params=pltpu.CompilerParams(vmem_limit_bytes=16 * 2**20),
        cost_estimate=pl.CostEstimate(flops=10**9, bytes_accessed=6 * 2**20, transcendentals=0),
    )(me, owner, pos, cot)


def forward_kernel(lane_ref, got_ref, weight_ref, rows_ref, part_ref, attn_ref, got):
    features = got.shape[1]
    capacity = rows_ref.shape[0]
    slots = got.shape[0] // got_ref.shape[0]
    block = attn_ref.shape[1]

    @pl.when(pl.program_id(0) == 0)
    def _():
        got[...] = got_ref[:, :slots].reshape(got.shape)
        attn_ref[:, :, :features] = got_ref[:, slots : slots + block]
        attn_ref[:, :, features:] = got_ref[:, slots + block :]

    row = lax.broadcasted_iota(jnp.int32, (capacity, got.shape[0]), 0)
    hit = row == lane_ref[0:1] - pl.program_id(0) * capacity
    rows = mm(jnp.where(hit, 1.0, 0.0).astype(BF16), got[...]).astype(BF16)
    rows_ref[...] = rows
    part_ref[...] = mm(rows, weight_ref[0]).astype(BF16)


def forward(lane, got, weight, rows):
    adapters, features, hidden = weight.shape
    received = lane.shape[1]
    capacity = rows // adapters
    slots = received // got.shape[0]
    attn = (got.shape[0], (got.shape[1] - slots) // 2, 2 * features)
    return pl.pallas_call(
        forward_kernel,
        grid=(adapters,),
        out_shape=(
            jax.ShapeDtypeStruct((rows, features), BF16),
            jax.ShapeDtypeStruct((rows, hidden), BF16),
            jax.ShapeDtypeStruct(attn, BF16),
        ),
        in_specs=[
            pl.BlockSpec((8, received), lambda a: (0, 0)),
            pl.BlockSpec(got.shape, lambda a: (0, 0, 0)),
            pl.BlockSpec((1, features, hidden), lambda a: (a, 0, 0)),
        ],
        out_specs=(
            pl.BlockSpec((capacity, features), lambda a: (a, 0)),
            pl.BlockSpec((capacity, hidden), lambda a: (a, 0)),
            pl.BlockSpec(attn, lambda a: (0, 0, 0)),
        ),
        scratch_shapes=[pltpu.VMEM((received, features), BF16)],
        compiler_params=pltpu.CompilerParams(vmem_limit_bytes=12 * 2**20),
        cost_estimate=pl.CostEstimate(flops=10**9, bytes_accessed=6 * 2**20, transcendentals=0),
    )(lane, got, weight)


def backward_kernel(
    pre_ref, bias_ref, out_ref, cot_ref, weight_ref, lane_ref,
    half_ref, bias_grad_ref, out_grad_ref, back_ref, reward_ref, unsort, grads,
):
    a = pl.program_id(0)
    capacity, hidden = pre_ref.shape
    features = weight_ref.shape[1]
    read_out = out_ref[0]
    pre = pre_ref[...].astype(F32) + bias_ref[0]
    s = 1.0 / (1.0 + jnp.exp(-pre))
    cot = jnp.concatenate([cot_ref[...].astype(F32)] * (hidden // 128), axis=1)
    activated = pre * s
    grad_pre = cot * read_out * s * (1.0 + pre * (1.0 - s))
    half = grad_pre.astype(BF16)
    half_ref[...] = half
    bias_grad_ref[0] = jnp.sum(grad_pre, axis=0, keepdims=True)
    out_grad_ref[0] = jnp.sum(cot * activated, axis=0, keepdims=True)
    reward = jnp.sum(activated * read_out, axis=1, keepdims=True)
    at = pl.ds(pl.multiple_of(a * capacity, capacity), capacity)
    grads[at, :features] = mm(half, weight_ref[0], NT).astype(BF16)
    grads[at, features:] = jnp.broadcast_to(reward, (capacity, 128)).astype(BF16)

    place = jnp.broadcast_to(lane_ref[0:1] + 1, (128, 128))
    lane = lax.broadcasted_iota(jnp.int32, (128, 128), 1)
    diagonal = lax.broadcasted_iota(jnp.int32, (128, 128), 0) == lane
    diagonal = jnp.where(diagonal, 1.0, 0.0).astype(BF16)
    high = (place // 32).astype(F32).astype(BF16)
    low = (place % 32).astype(F32).astype(BF16)
    row = mm(diagonal, high, NT) * 32.0 + mm(diagonal, low, NT)
    row = row.astype(jnp.int32) - 1
    part = pl.ds(pl.multiple_of(a * 128, 128), 128)
    for n in range(0, unsort.shape[1], 128):
        unsort[part, n : n + 128] = jnp.where(row - n == lane, 1.0, 0.0).astype(BF16)

    @pl.when(a == pl.num_programs(0) - 1)
    def _():
        back = mm(unsort[...], grads[...]).astype(BF16)
        back_ref[...] = back[:, :features]
        first = lax.broadcasted_iota(jnp.int32, (16, 128), 1) == 0
        first = jnp.where(first, 1.0, 0.0).astype(BF16)
        reward_ref[...] = mm(first, back[:, features:], NT).astype(BF16)


def backward(pre, bias, read_out, cot, weight, lane):
    adapters, features, hidden = weight.shape
    received, rows = lane.shape[1], pre.shape[0]
    capacity = rows // adapters
    line = pl.BlockSpec((1, 1, hidden), lambda a: (a, 0, 0))
    half, bias_grad, out_grad, back, reward = pl.pallas_call(
        backward_kernel,
        grid=(adapters,),
        out_shape=(
            jax.ShapeDtypeStruct((rows, hidden), BF16),
            jax.ShapeDtypeStruct((adapters, 1, hidden), F32),
            jax.ShapeDtypeStruct((adapters, 1, hidden), F32),
            jax.ShapeDtypeStruct((received, features), BF16),
            jax.ShapeDtypeStruct((16, received), BF16),
        ),
        in_specs=[
            pl.BlockSpec((capacity, hidden), lambda a: (a, 0)),
            line,
            line,
            pl.BlockSpec((capacity, 128), lambda a: (a, 0)),
            pl.BlockSpec((1, features, hidden), lambda a: (a, 0, 0)),
            pl.BlockSpec((8, 128), lambda a: (0, a)),
        ],
        out_specs=(
            pl.BlockSpec((capacity, hidden), lambda a: (a, 0)),
            line,
            line,
            pl.BlockSpec((received, features), lambda a: (0, 0)),
            pl.BlockSpec((16, received), lambda a: (0, 0)),
        ),
        scratch_shapes=[
            pltpu.VMEM((received, rows), BF16),
            pltpu.VMEM((rows, features + 128), BF16),
        ],
        compiler_params=pltpu.CompilerParams(vmem_limit_bytes=16 * 2**20),
        cost_estimate=pl.CostEstimate(flops=10**9, bytes_accessed=8 * 2**20, transcendentals=2**19),
    )(pre, bias[:, None], read_out[:, None], cot, weight, lane)
    return half, bias_grad[:, 0], out_grad[:, 0], back, reward


def pick_kernel(pick_ref, group_ref, attn_ref, out_ref):
    owners, height, features = out_ref.shape
    block = attn_ref.shape[0]
    slots = height - 2 * block
    chosen = pick_ref[0] + pick_ref[1]
    out = mm(chosen, group_ref[...]).astype(BF16)
    out_ref[:, :slots] = out.reshape(owners, slots, features)
    for o in range(owners):
        start = 2 * o * features
        left = attn_ref[:, start : start + features]
        right = attn_ref[:, start + features : start + 2 * features]
        out_ref[o, slots:] = jnp.concatenate([left, right], axis=0)


def call(kernel, outs, mflops, mbytes, *args):
    vmem = pl.BlockSpec(memory_space=pltpu.VMEM)
    smem = pl.BlockSpec(memory_space=pltpu.SMEM)
    return pl.pallas_call(
        kernel,
        out_shape=tuple(jax.ShapeDtypeStruct(shape, dtype) for shape, dtype in outs),
        in_specs=[smem if arg.ndim == 1 else vmem for arg in args],
        out_specs=tuple(vmem for _ in outs),
        compiler_params=pltpu.CompilerParams(vmem_limit_bytes=12 * 2**20),
        cost_estimate=pl.CostEstimate(
            flops=mflops * 10**6, bytes_accessed=mbytes * 2**20, transcendentals=0
        ),
    )(*args)


def local(
    hidden_states, attn_input, rule_ids, slot_ids, cotangent, adapter_in, adapter_bias, adapter_out
):
    dp_size = lax.axis_size("dp")
    rule_size = lax.axis_size("rule")
    block = hidden_states.shape[0]
    adapters, feature_cols, hidden_units = adapter_in.shape
    tokens = block * rule_size
    capacity = 4 * block * rule_size // adapters
    rows = adapters * capacity
    slots = 2 * rule_size

    group_rows = lax.all_to_all(hidden_states, "rule", split_axis=1, concat_axis=0, tiled=True)

    rule_all = rule_ids.T.reshape(2, dp_size, tokens)
    slot_all = slot_ids.T.reshape(2, dp_size, tokens)
    cot_all = cotangent.T.reshape(2, dp_size, tokens)
    owner = rule_all // adapters
    pos = jnp.where(slot_all >= 0, rule_all % adapters * capacity + slot_all, -1)
    me = lax.axis_index("dp").astype(jnp.int32).reshape(1)
    lane, pick, cot_rows = tables(block, rows, me, owner, pos, cot_all)
    (outgoing,) = call(
        pick_kernel, [((dp_size, slots + 2 * block, feature_cols), BF16)], 200, 2,
        pick, group_rows, attn_input,
    )
    got = lax.all_to_all(outgoing, "dp", split_axis=0, concat_axis=0, tiled=True)
    rows_buf, partial_pre, attn_cols = forward(lane, got, adapter_in, rows)
    attn_all = lax.all_gather(attn_cols, "rule", axis=1, tiled=True)
    shares = lax.all_to_all(partial_pre, "rule", split_axis=0, concat_axis=0, tiled=True)
    share = jnp.sum(
        shares.reshape(rule_size, rows // rule_size, hidden_units).astype(F32), axis=0
    ).astype(BF16)
    share = jnp.broadcast_to(share[None], (rule_size,) + share.shape).reshape(rows, hidden_units)
    preact = lax.all_to_all(share, "rule", split_axis=0, concat_axis=0, tiled=True)

    grad_half, bias_grad, out_grad, back, reward = backward(
        preact, adapter_bias, adapter_out, cot_rows, adapter_in, lane
    )
    returned = lax.all_to_all(back, "dp", split_axis=0, concat_axis=0, tiled=True)
    state_grad = mm(pick[0] + pick[1], returned, TN).astype(BF16)
    attn_all, state_grad = lax.optimization_barrier((attn_all, state_grad))
    cut = tokens // 2 - 8
    width = attn_all.shape[2]
    attn_low = attn_all[:, :cut].reshape(dp_size * cut, width)
    attn_high = attn_all[:, cut:].reshape(dp_size * (tokens - cut), width)
    state_low = lax.all_gather(state_grad[:cut], "dp", axis=0, tiled=True)
    state_high = lax.all_gather(state_grad[cut:], "dp", axis=0, tiled=True)

    reward_back = lax.all_to_all(
        reward[0].reshape(dp_size, slots), "dp", split_axis=0, concat_axis=0, tiled=True
    )
    rewards = lax.dot_general(
        pick, reward_back.reshape(-1), (((1,), (0,)), ((), ())), preferred_element_type=F32
    )
    rewards = rewards.astype(BF16).T
    in_grad = jnp.einsum(
        "acd,acr->adr",
        rows_buf.reshape(adapters, capacity, feature_cols),
        grad_half.reshape(adapters, capacity, hidden_units),
        preferred_element_type=F32,
    ).astype(BF16)
    o_proj_grad = mm(state_low, attn_low, TN) + mm(state_high, attn_high, TN)
    o_proj_grad = o_proj_grad.astype(BF16)
    return (rewards, in_grad, bias_grad, out_grad, o_proj_grad)


def solution(mesh):
    placed = (
        P(("dp", "rule"), None),
        P(("dp", "rule"), None),
        P(),
        P(),
        P(),
        P("dp", "rule", None),
        P("dp", None),
        P("dp", None),
    )
    return jax.shard_map(
        local,
        mesh=mesh,
        in_specs=placed,
        out_specs=(
            P("dp", None),
            P("dp", "rule", None),
            P("dp", None),
            P("dp", None),
            P("rule", "dp"),
        ),
        check_vma=False,
    )
```
